32 devices in a mesh: kv: 2 (over y), ex: 16 (over z, x, core).
Axes of the slice: x: 2, y: 2, z: 4, core: 2. Of those that a mesh axis runs over, the one named last changes fastest.
Arguments:
- x_tokens: bfloat16 [16, 576, 2048], P('ex'), may hold values from -6 to 6
- attn_gain: float32 [2048], replicated, may hold values from 0.1 to 1.9
- w_qkv: bfloat16 [2048, 3, 2048], P(None, None, 'kv'), may hold values from -1 to 1
- w_out: bfloat16 [2048, 2048], P('kv'), may hold values from -0.125 to 0.125
- cache: bfloat16 [32, 2, 512, 2048], P('ex', None, None, 'kv'), may hold values from -6 to 6
- cache_len: int32 [32], P('ex'), may hold values from 1 to 512, 8192 in all
- moe_gain: float32 [2048], replicated, may hold values from 0.1 to 1.9
- w_trainer: float32 [16, 3, 2048, 1024], P(None, None, 'ex', 'kv'), may hold values from -0.125 to 0.125
- expert_ids: int32 [16, 576, 8], P('ex', 'kv'), may hold values from 0 to 15, all different within a row; in each aligned block of 288 rows (0 to 287, 288 to 575, ..., all dimensions but the last counted through in order) at most 230 rows name the same one
- route_probs: float32 [16, 576, 8], P('ex', 'kv'), may hold values from 0.05 to 1
Outputs:
- layer_out: bfloat16 [16, 576, 2048], P('ex', 'kv')
The draws below stay inside these ranges and needn't reach their ends.
Inputs may be any that keep to these rules, and one draw needn't show every extreme that they name: `expert_ids`: in each aligned block of 288 tokens, no expert is named by more than 230 of them; each token names 8 different experts.
All inputs are finite; a program needn't handle non-finite values. No bound on the sum of `cache_len` on one device may be relied on, other than what follows from the above.
Results may differ from the reference program's by a relative error of at most 0.0055.
Values may be sent and summed in bfloat16 or wider, within the bound.
No kernel may reach another device: no remote copies, remote signals or barrier semaphores. Data moves between devices by JAX's collectives and lax.ppermute only.
A program may use at most 192 MiB of HBM per device.

```python
import math
import jax
import jax.numpy as jnp
import numpy as np
from jax import lax

D = 2048
H = 16
HD = 128
FF = 1024
TOPK = 8
PLEN = 512
REQ_DEV = 2
QB = 32
CMAX = 512
EXPERTS = 16
GROUPS = 16
REQUESTS = 32
ROWS = 576
ROWS_DEV = 288
CAP = 230


def draw_w_qkv(key, part):
    base = jax.random.normal(key, (D, 3, H * HD), jnp.float32) / math.sqrt(D)
    return jnp.clip(base, -1.0, 1.0).astype(jnp.bfloat16)


def levels(key, shape, shards, least, top_value):
    def one(dim, shards_of):
        draws = jax.random.uniform(jax.random.fold_in(jax.random.fold_in(key, 6), dim), (shards_of,), jnp.float32, least / len(shards), top_value / len(shards))
        return jnp.repeat(jnp.exp(draws), shape[dim] // shards_of).reshape((-1,) + (1,) * (len(shape) - dim - 1))

    level = one(*shards[0])
    for cut in shards[1:]:
        level = level * one(*cut)
    return level


def profile(number_of, total, bound, slope):
    loads = [(1 << 20) // math.isqrt(standing ** slope) + 1 for standing in range(2, number_of + 1)]
    spare, given = total - bound - (number_of - 1), [1] * (number_of - 1)
    while spare > 0:
        free = [i for i in range(number_of - 1) if given[i] < bound]
        pool, remaining = sum([loads[i] for i in free]), spare
        for i in free:
            addition = min(bound - given[i], max(1, remaining * loads[i] // pool), spare)
            given[i] = given[i] + addition
            spare = spare - addition
    return np.array([bound] + given)


def ragged(own_key, count, total, reach, lean):
    if count == 2:
        one = jax.random.randint(own_key, (), max(1, total - reach), min(reach, total - 1) + 1)
        return jnp.stack([one, total - one])
    sizes = jnp.asarray(profile(count, total, reach, lean), jnp.int32)
    couples = (count - 1) // 2
    giver, taker = sizes[1:1 + 2 * couples:2], sizes[2:2 + 2 * couples:2]
    room = jnp.minimum(giver - 1, reach - taker)
    shifted = jax.random.randint(jax.random.fold_in(own_key, 1), (couples,), 0, 1 << 20) % (room + 1)
    sizes = sizes.at[1:1 + 2 * couples:2].set(giver - shifted).at[2:2 + 2 * couples:2].set(taker + shifted)
    return sizes[jax.random.permutation(jax.random.fold_in(own_key, 2), count)]


def shared_out(own_key, own, number, rows, count, top, limit, lean):
    sequence = jax.random.permutation(own_key, count)
    packed, usual = portions_of(count, rows * top, limit, lean, True), portions_of(count, rows * top, limit, lean, False)
    places = jnp.arange(count)

    def named(tallies, turn):
        used = int((tallies > 0).sum())
        fixed = max(1, used // 4)
        passed = fixed + (places - fixed + turn * (used - fixed)) % max(1, count - fixed)
        return jnp.zeros((count,), jnp.int32).at[sequence[jnp.where(places < fixed, places, passed)]].set(jnp.asarray(tallies, jnp.int32))

    tallies = jnp.where(number % 4 == 0, named(packed, number // 4), named(usual, number - number // 4 - 1))
    mixed = jax.random.permutation(jax.random.fold_in(own, 3), count)
    source_of, sink = mixed[0:count // 2 * 2:2], mixed[1:count // 2 * 2:2]
    slack = jnp.minimum(tallies[source_of] - 1, limit - tallies[sink]) // 2
    slack = jnp.where((source_of == sequence[0]) | (sink == sequence[0]) | (tallies[sink] == 0), 0, jnp.maximum(slack, 0))
    passed = jax.random.randint(jax.random.fold_in(own, 4), (count // 2,), 0, 1 << 20) % (slack + 1)
    tallies = tallies.at[source_of].add(-passed).at[sink].add(passed)
    members = jnp.searchsorted(jnp.cumsum(tallies), jnp.arange(rows * top), side="right").astype(jnp.int32)
    table = members.reshape(top, rows).T
    table = table[jax.random.permutation(jax.random.fold_in(own, 1), rows)]
    turn = jax.random.randint(jax.random.fold_in(own, 2), (rows, 1), 0, top)
    return jnp.take_along_axis(table, (jnp.arange(top)[None, :] + turn) % top, axis=1)


def portions_of(amount, total, bound, lean, full):
    loads = [(1 << 20) // math.isqrt(grade ** lean) + 1 for grade in range(1, amount + 1)]
    largest = bound if full else min(bound, max(-(-total // amount), total * loads[0] // sum(loads)))
    least = 1 if total - largest >= amount - 1 else 0
    given, surplus = [largest] + [least] * (amount - 1), total - largest - least * (amount - 1)
    while surplus > 0:
        candidates = [i for i in range(1, amount) if given[i] < largest] or [i for i in range(1, amount) if given[i] < bound]
        pool, budget = sum([loads[i] for i in candidates]), surplus
        for i in candidates:
            more = min(bound - given[i], max(1, budget * loads[i] // pool), surplus)
            given[i] = given[i] + more
            surplus = surplus - more
    return np.array(given)


def noise(stream_key, extent, deviation, reach, split=(), kind=jnp.bfloat16):
    entries = jax.random.normal(stream_key, extent, jnp.float32) * deviation
    if len(split) > 0:
        entries = levels(stream_key, extent, split, -0.22, 0.18) * entries
    return jnp.clip(entries, min=-reach, max=reach).astype(kind)


def setup_inputs(seed: int = 0) -> dict:
    arg_keys = jax.random.split(jax.random.key(seed), 11)
    x_tokens = noise(arg_keys[0], (GROUPS, ROWS, D), 1.0, 6.0, ((0, 16),))
    attn_gain = jnp.clip(1.0 + 0.18 * jax.random.normal(arg_keys[1], (D,), jnp.float32), 0.1, 1.9)
    w_qkv = draw_w_qkv(jax.random.fold_in(arg_keys[10], 71), 0)
    w_out = noise(arg_keys[3], (H * HD, D), (H * HD) ** -0.5, 0.125, ((0, 2),))
    cache = noise(arg_keys[4], (REQUESTS, 2, CMAX, H * HD), 1.0, 6.0, ((0, 16), (3, 2)))
    cache_len = ragged(arg_keys[5], REQUESTS, REQUESTS * CMAX // 2, CMAX, 2).astype(jnp.int32)
    moe_gain = jnp.clip(1.0 + 0.18 * jax.random.normal(arg_keys[6], (D,), jnp.float32), 0.1, 1.9)
    w_trainer = noise(arg_keys[7], (EXPERTS, 3, D, FF), D ** -0.5, 0.125, ((2, 16), (3, 2)), jnp.float32)
    expert_ids_keys = jax.random.split(jax.random.fold_in(arg_keys[8], 1), GROUPS * ROWS // ROWS_DEV)
    expert_ids_turns = jax.random.permutation(jax.random.fold_in(arg_keys[8], 3), GROUPS * ROWS // ROWS_DEV)
    expert_ids = jax.vmap(lambda own, number: shared_out(jax.random.fold_in(arg_keys[8], 2), own, number, ROWS_DEV, EXPERTS, TOPK, CAP, 2))(expert_ids_keys, expert_ids_turns).reshape((GROUPS, ROWS, TOPK))
    route_probs = jnp.clip(jnp.exp(math.log(1.0) - 2.9957323 * jax.random.uniform(arg_keys[9], (GROUPS, ROWS, TOPK), jnp.float32) ** levels(arg_keys[9], (GROUPS, ROWS, TOPK), ((0, 16), (1, 2)), -0.2, 0.2)), 0.05, 1.0)
    return dict(x_tokens=x_tokens, attn_gain=attn_gain, w_qkv=w_qkv, w_out=w_out, cache=cache, cache_len=cache_len, moe_gain=moe_gain, w_trainer=w_trainer, expert_ids=expert_ids, route_probs=route_probs)


block_rows = 512

def rms_scale(rows, gain):
    values = rows.astype(jnp.float32)
    scale = lax.rsqrt(lax.optimization_barrier(jnp.mean(values * values, axis=-1, keepdims=True)) + 1e-06)
    return values * scale * gain.astype(jnp.float32)

def attend(query, keys, values, valid):
    scores = jnp.einsum('qhd,khd->hqk', query.astype(jnp.float32), keys.astype(jnp.float32)) / math.sqrt(HD)
    scores = jnp.where(valid[None, None, :], scores, -1e+30)
    top = lax.optimization_barrier(jnp.max(scores, axis=-1, keepdims=True))
    weights = jnp.exp(scores - top)
    probs = (weights / lax.optimization_barrier(jnp.sum(weights, axis=-1, keepdims=True))).astype(jnp.bfloat16)
    mixed = jnp.einsum('hqk,khd->qhd', probs.astype(jnp.float32), values.astype(jnp.float32))
    return mixed.astype(jnp.bfloat16)

def reference(x_tokens, attn_gain, w_qkv, w_out, cache, cache_len, moe_gain, w_trainer, expert_ids, route_probs):
    server = w_trainer.astype(jnp.bfloat16)
    flat_qkv = w_qkv.reshape(D, 3 * H * HD)
    lengths_all = cache_len.reshape(GROUPS, REQ_DEV)
    stores = cache.reshape(GROUPS, REQ_DEV, 2, CMAX, H * HD)

    def group(items):
        rows, lengths, store = items
        normed = rms_scale(rows, attn_gain).astype(jnp.bfloat16)
        proj = jnp.dot(normed, flat_qkv, preferred_element_type=jnp.float32).astype(jnp.bfloat16)
        proj = proj.reshape(ROWS, 3, H, HD)
        query, keys, values = (proj[:, 0], proj[:, 1], proj[:, 2])
        prompt_out = attend(query[:PLEN], keys[:PLEN], values[:PLEN], jnp.ones((PLEN,), dtype=bool))
        req_q = query[PLEN:].reshape(REQ_DEV, QB, H, HD)
        req_k = keys[PLEN:].reshape(REQ_DEV, QB, H, HD)
        req_v = values[PLEN:].reshape(REQ_DEV, QB, H, HD)
        all_k = jnp.concatenate([req_k, store[:, 0].reshape(REQ_DEV, CMAX, H, HD)], axis=1)
        all_v = jnp.concatenate([req_v, store[:, 1].reshape(REQ_DEV, CMAX, H, HD)], axis=1)
        live = jnp.arange(CMAX, dtype=jnp.int32)[None, :] < lengths[:, None]
        valid = jnp.concatenate([jnp.ones((REQ_DEV, QB), dtype=bool), live], axis=1)
        req_out = jax.vmap(attend)(req_q, all_k, all_v, valid)
        heads_out = jnp.concatenate([prompt_out, req_out.reshape(REQ_DEV * QB, H, HD)], axis=0)
        heads_out = heads_out.reshape(ROWS, H * HD)
        attn = jnp.dot(heads_out, w_out, preferred_element_type=jnp.float32)
        return rows.astype(jnp.float32) + attn
    resid = lax.map(group, (x_tokens, lengths_all, stores))
    flat_res = resid.reshape(GROUPS * ROWS, D)
    moe_in = rms_scale(flat_res, moe_gain).astype(jnp.bfloat16)
    probs = route_probs.reshape(-1, TOPK)
    share = (probs / lax.optimization_barrier(jnp.sum(probs, axis=-1, keepdims=True))).reshape(-1)
    keys_flat = expert_ids.reshape(-1).astype(jnp.int32)
    order = jnp.argsort(keys_flat, stable=True).astype(jnp.int32)
    counts = lax.optimization_barrier(jnp.sum((keys_flat[:, None] == jnp.arange(EXPERTS, dtype=jnp.int32)[None, :]).astype(jnp.int32), axis=0))
    starts = (jnp.cumsum(counts) - counts).astype(jnp.int32)
    order_pad = jnp.concatenate([order, jnp.zeros((block_rows,), jnp.int32)])

    def expert_step(expert, total):
        weights = server[expert]

        def block_step(index, total):
            begin = (starts[expert] + index * block_rows).astype(jnp.int32)
            picks = lax.dynamic_slice(order_pad, (begin,), (block_rows,))
            live = index * block_rows + jnp.arange(block_rows, dtype=jnp.int32) < counts[expert]
            tokens = picks // TOPK
            rows = moe_in[tokens]
            gate = jnp.dot(rows, weights[0], preferred_element_type=jnp.float32)
            up = jnp.dot(rows, weights[1], preferred_element_type=jnp.float32)
            hidden = (jax.nn.silu(gate) * up).astype(jnp.bfloat16)
            result = lax.dot_general(hidden, weights[2], (((1,), (1,)), ((), ())), preferred_element_type=jnp.float32)
            result = result.astype(jnp.bfloat16)
            factor = jnp.where(live, share[picks], jnp.zeros((block_rows,), jnp.float32))
            return total.at[tokens].add(factor[:, None] * result.astype(jnp.float32))
        blocks = (counts[expert] + block_rows - 1) // block_rows
        return lax.fori_loop(0, blocks, block_step, total)
    total = lax.fori_loop(0, EXPERTS, expert_step, jnp.zeros((GROUPS * ROWS, D), jnp.float32))
    return (flat_res + total).astype(jnp.bfloat16).reshape(GROUPS, ROWS, D)
```

```python
import functools
import math

import jax
import jax.numpy as jnp
from jax import lax
from jax.experimental import pallas as pl
from jax.experimental.pallas import tpu as pltpu
from jax.sharding import PartitionSpec as P

HD = 128
TOPK = 8
PLEN = 512
REQ_DEV = 2
QB = 32
CMAX = 512


def rms_scale(rows, gain):
    values = rows.astype(jnp.float32)
    scale = lax.rsqrt(jnp.mean(values * values, axis=-1, keepdims=True) + 1e-06)
    return values * scale * gain


def attend(query, keys, values, valid):
    scores = jnp.einsum(
        "qhd,khd->hqk", query, keys, preferred_element_type=jnp.float32
    ) / math.sqrt(HD)
    scores = jnp.where(valid[None, None, :], scores, -1e30)
    top = jnp.max(scores, axis=-1, keepdims=True)
    weights = jnp.exp(scores - top)
    probs = (weights / jnp.sum(weights, axis=-1, keepdims=True)).astype(jnp.bfloat16)
    mixed = jnp.einsum("hqk,khd->qhd", probs, values, preferred_element_type=jnp.float32)
    return mixed.astype(jnp.bfloat16)


def ffn_kernel(parts, x_ref, share_ref, *refs):
    out_ref = refs[-1]
    width = x_ref.shape[1]
    x = x_ref[...]
    total = None
    for part in range(parts):
        gate_w, up_w, down_w = (r[...].reshape(width, r.shape[-1]) for r in refs[3 * part : 3 * part + 3])
        gate = jnp.dot(x, gate_w, preferred_element_type=jnp.float32)
        up = jnp.dot(x, up_w, preferred_element_type=jnp.float32)
        hidden = (gate * jax.nn.sigmoid(gate) * up).astype(jnp.bfloat16)
        term = lax.dot_general(
            hidden, down_w, (((1,), (1,)), ((), ())), preferred_element_type=jnp.float32
        )
        total = term if total is None else total + term
    out_ref[...] = (total * share_ref[...]).astype(jnp.bfloat16)


def row_block(rows):
    for block in (384, 288, 256, 192, 144, 128, 96, 64, 48, 32, 16):
        if rows % block == 0:
            return block
    return rows


def expert_ffn(rows, share, weights):
    count, width = rows.shape
    block = row_block(count)
    parts = len(weights) // 3
    whole = [
        pl.BlockSpec(w.shape, lambda i, n=w.ndim: (0,) * n, pipeline_mode=pl.Buffered(1))
        for w in weights
    ]
    hidden = sum(w.shape[-1] for w in weights) // 3
    return pl.pallas_call(
        functools.partial(ffn_kernel, parts),
        grid=(count // block,),
        in_specs=[
            pl.BlockSpec((block, width), lambda i: (i, 0)),
            pl.BlockSpec((block, 1), lambda i: (i, 0)),
        ]
        + whole,
        out_specs=pl.BlockSpec((block, width), lambda i: (i, 0)),
        out_shape=jax.ShapeDtypeStruct((count, width), jnp.bfloat16),
        compiler_params=pltpu.CompilerParams(vmem_limit_bytes=50 * 1024 * 1024),
        cost_estimate=pl.CostEstimate(
            flops=6 * count * width * hidden,
            bytes_accessed=4 * count * width + 6 * width * hidden,
            transcendentals=count * hidden,
        ),
        name="expert_ffn",
    )(rows, share, *weights)


def chunks_of(rows, most):
    for number in range(most, 1, -1):
        if rows % number == 0 and (rows // number) % 16 == 0:
            return number
    return 1


def on_device(
    x_tokens,
    attn_gain,
    w_qkv,
    w_out,
    cache,
    cache_len,
    moe_gain,
    w_trainer,
    expert_ids,
    route_probs,
):
    kv = lax.axis_size("kv")
    experts = w_trainer.shape[0]
    mine = []
    for kind in range(3):
        part = w_trainer[:, kind].astype(jnp.bfloat16)
        mine.append(lax.all_to_all(part, "ex", split_axis=0, concat_axis=0, tiled=True))
    weights = list(mine)
    for step in range(1, kv):
        turn = [(i, (i + step) % kv) for i in range(kv)]
        weights += [lax.ppermute(w, "kv", turn) for w in mine]

    probs = route_probs[0]
    share = probs / jnp.sum(probs, axis=-1, keepdims=True)
    named = expert_ids[0][:, :, None] == jnp.arange(experts, dtype=jnp.int32)[None, None, :]
    factor = jnp.sum(jnp.where(named, share[:, :, None], 0.0), axis=1)
    factor = lax.all_to_all(factor.T, "ex", split_axis=0, concat_axis=0, tiled=True)

    rows = x_tokens[0]
    row_count = rows.shape[0]
    local_heads = w_qkv.shape[2] // HD
    normed = rms_scale(rows, attn_gain).astype(jnp.bfloat16)
    query, keys, values = (
        jnp.dot(normed, w_qkv[:, j], preferred_element_type=jnp.float32)
        .astype(jnp.bfloat16)
        .reshape(row_count, local_heads, HD)
        for j in range(3)
    )
    prompt_out = attend(query[:PLEN], keys[:PLEN], values[:PLEN], jnp.ones((PLEN,), dtype=bool))
    req_q = query[PLEN:].reshape(REQ_DEV, QB, local_heads, HD)
    req_k = keys[PLEN:].reshape(REQ_DEV, QB, local_heads, HD)
    req_v = values[PLEN:].reshape(REQ_DEV, QB, local_heads, HD)
    all_k = jnp.concatenate([req_k, cache[:, 0].reshape(REQ_DEV, CMAX, local_heads, HD)], axis=1)
    all_v = jnp.concatenate([req_v, cache[:, 1].reshape(REQ_DEV, CMAX, local_heads, HD)], axis=1)
    live = jnp.arange(CMAX, dtype=jnp.int32)[None, :] < cache_len[:, None]
    valid = jnp.concatenate([jnp.ones((REQ_DEV, QB), dtype=bool), live], axis=1)
    req_out = jax.vmap(attend)(req_q, all_k, all_v, valid)
    heads_out = jnp.concatenate(
        [prompt_out, req_out.reshape(REQ_DEV * QB, local_heads, HD)], axis=0
    )
    heads_out = heads_out.reshape(row_count, local_heads * HD)
    rows_dev = row_count // kv
    mixed = lax.psum_scatter(
        jnp.dot(heads_out, w_out, preferred_element_type=jnp.float32),
        "kv",
        scatter_dimension=0,
        tiled=True,
    )
    own_rows = lax.dynamic_slice_in_dim(rows, lax.axis_index("kv") * rows_dev, rows_dev, 0)
    resid = own_rows.astype(jnp.float32) + mixed
    moe_in = rms_scale(resid, moe_gain).astype(jnp.bfloat16)

    number = chunks_of(rows_dev, 2)
    size = rows_dev // number
    outs = []
    for c in range(number):
        cut = slice(c * size, (c + 1) * size)
        gathered = lax.all_gather(moe_in[cut], "ex", axis=0, tiled=True)
        done = expert_ffn(gathered, factor[:, cut].reshape(-1, 1), weights)
        back = lax.psum_scatter(done, "ex", scatter_dimension=0, tiled=True)
        outs.append((resid[cut] + back.astype(jnp.float32)).astype(jnp.bfloat16))
    return jnp.concatenate(outs, axis=0)[None]


def solution(mesh):
    return jax.shard_map(
        on_device,
        mesh=mesh,
        in_specs=(
            P("ex", None, None),
            P(),
            P(None, None, "kv"),
            P("kv", None),
            P("ex", None, None, "kv"),
            P("ex"),
            P(),
            P(None, None, "ex", "kv"),
            P("ex", "kv", None),
            P("ex", "kv", None),
        ),
        out_specs=P("ex", "kv", None),
        check_vma=False,
    )
```

```python
import math

import jax
import jax.numpy as jnp
import numpy as np
from jax import lax
from jax.experimental import pallas as pl
from jax.experimental.pallas import tpu as pltpu
from jax.sharding import PartitionSpec as P

HD = 128
TOPK = 8
PLEN = 512
REQ_DEV = 2
QB = 32
CMAX = 512


def rms_scale(rows, gain):
    values = rows.astype(jnp.float32)
    scale = lax.rsqrt(jnp.mean(values * values, axis=-1, keepdims=True) + 1e-06)
    return values * scale * gain


def attend(query, keys, values, valid):
    scores = jnp.einsum(
        "qhd,khd->hqk", query, keys, preferred_element_type=jnp.float32
    ) / math.sqrt(HD)
    scores = jnp.where(valid[None, None, :], scores, -1e30)
    top = jnp.max(scores, axis=-1, keepdims=True)
    weights = jnp.exp(scores - top)
    probs = (weights / jnp.sum(weights, axis=-1, keepdims=True)).astype(jnp.bfloat16)
    mixed = jnp.einsum("hqk,khd->qhd", probs, values, preferred_element_type=jnp.float32)
    return mixed.astype(jnp.bfloat16)


def ffn_kernel(pieces, parts, cuts, refs):
    x_refs, share_ref = refs[:pieces], refs[pieces]
    weight_refs = refs[pieces + 1 : -4]
    keep_ref, give_ref, x_all, total = refs[-4:]
    step = pl.program_id(0)
    width = x_all.shape[1]

    @pl.when(step == 0)
    def _():
        size = x_refs[0].shape[0]
        for i in range(pieces):
            x_all[i * size : (i + 1) * size] = x_refs[i][...]
        total[...] = jnp.zeros_like(total)

    for part in range(parts):

        @pl.when(step // cuts == part)
        def _():
            x = x_all[...]
            gate_w, up_w, down_w = (
                r[...].reshape(width, r.shape[-1]) for r in weight_refs[3 * part : 3 * part + 3]
            )
            gate = jnp.dot(x, gate_w, preferred_element_type=jnp.float32)
            up = jnp.dot(x, up_w, preferred_element_type=jnp.float32)
            hidden = (gate * jax.nn.sigmoid(gate) * up).astype(jnp.bfloat16)
            total[...] += lax.dot_general(
                hidden, down_w, (((1,), (1,)), ((), ())), preferred_element_type=jnp.float32
            )

    @pl.when(step == parts * cuts - 1)
    def _():
        half = keep_ref.shape[0]
        keep_ref[...] = (total[:half] * share_ref[:half]).astype(jnp.bfloat16)
        give_ref[...] = (total[half:] * share_ref[half:]).astype(jnp.bfloat16)


def expert_ffn(blocks, share, weights):
    half, width = blocks[0].shape
    if half % 16:
        blocks = [jnp.concatenate(blocks, axis=0)]
    pieces = len(blocks)
    count = 2 * half
    parts = len(weights) // 3
    sources, slice_width, units = weights[0].shape
    unit_block = min(256, units)
    cuts = units // unit_block
    hidden = parts * units

    def weight_spec(part):
        return pl.BlockSpec(
            (sources, slice_width, unit_block),
            lambda i: (0, 0, jnp.clip(i - part * cuts, 0, cuts - 1)),
        )

    out = jax.ShapeDtypeStruct((half, width), jnp.bfloat16)
    return pl.pallas_call(
        lambda *refs: ffn_kernel(pieces, parts, cuts, refs),
        grid=(parts * cuts,),
        in_specs=[pl.BlockSpec(blocks[0].shape, lambda i: (0, 0))] * pieces
        + [pl.BlockSpec((count, 1), lambda i: (0, 0))]
        + [weight_spec(part) for part in range(parts) for kind in range(3)],
        out_specs=[pl.BlockSpec((half, width), lambda i: (0, 0))] * 2,
        out_shape=[out, out],
        scratch_shapes=[
            pltpu.VMEM((count, width), jnp.bfloat16),
            pltpu.VMEM((count, width), jnp.float32),
        ],
        compiler_params=pltpu.CompilerParams(vmem_limit_bytes=44 * 1024 * 1024),
        cost_estimate=pl.CostEstimate(
            flops=6 * count * width * hidden,
            bytes_accessed=4 * count * width + 6 * width * hidden,
            transcendentals=count * hidden,
        ),
        name="expert_ffn",
    )(*blocks, share, *weights)


def chip_ring(chips):
    rows = 4
    columns = chips // rows
    if chips % rows or columns < 2:
        return list(range(chips))
    order = [z * columns for z in range(rows)]
    for turn, z in enumerate(reversed(range(rows))):
        line = [z * columns + x for x in range(1, columns)]
        order += line if turn % 2 == 0 else line[::-1]
    return order


def on_device(
    x_tokens,
    attn_gain,
    w_qkv,
    w_out,
    cache,
    cache_len,
    moe_gain,
    w_trainer,
    expert_ids,
    route_probs,
):
    kv, ex = lax.axis_size("kv"), lax.axis_size("ex")
    me, me_kv = lax.axis_index("ex"), lax.axis_index("kv")
    experts = w_trainer.shape[0]

    mine = []
    for kind in range(3):
        part = w_trainer[:, kind].astype(jnp.bfloat16)
        mine.append(lax.all_to_all(part, "ex", split_axis=0, concat_axis=0, tiled=True))
    weights = list(mine)
    for turn in range(1, kv):
        weights += [
            lax.ppermute(w, "kv", [(i, (i + turn) % kv) for i in range(kv)]) for w in mine
        ]

    probs = route_probs[0]
    share = probs / jnp.sum(probs, axis=-1, keepdims=True)
    named = expert_ids[0][:, :, None] == jnp.arange(experts, dtype=jnp.int32)[None, None, :]
    factor = jnp.sum(jnp.where(named, share[:, :, None], 0.0), axis=1)
    factor = lax.all_gather(factor, "ex", axis=0)
    factor = jnp.sum(jnp.where(jnp.arange(experts) == me, factor, 0.0), axis=-1)

    rows = x_tokens[0]
    row_count = rows.shape[0]
    local_heads = w_qkv.shape[2] // HD
    normed = rms_scale(rows, attn_gain).astype(jnp.bfloat16)
    query, keys, values = (
        jnp.dot(normed, w_qkv[:, j], preferred_element_type=jnp.float32)
        .astype(jnp.bfloat16)
        .reshape(row_count, local_heads, HD)
        for j in range(3)
    )
    prompt_out = attend(query[:PLEN], keys[:PLEN], values[:PLEN], jnp.ones((PLEN,), dtype=bool))
    req_q = query[PLEN:].reshape(REQ_DEV, QB, local_heads, HD)
    req_k = keys[PLEN:].reshape(REQ_DEV, QB, local_heads, HD)
    req_v = values[PLEN:].reshape(REQ_DEV, QB, local_heads, HD)
    all_k = jnp.concatenate([req_k, cache[:, 0].reshape(REQ_DEV, CMAX, local_heads, HD)], axis=1)
    all_v = jnp.concatenate([req_v, cache[:, 1].reshape(REQ_DEV, CMAX, local_heads, HD)], axis=1)
    live = jnp.arange(CMAX, dtype=jnp.int32)[None, :] < cache_len[:, None]
    valid = jnp.concatenate([jnp.ones((REQ_DEV, QB), dtype=bool), live], axis=1)
    req_out = jax.vmap(attend)(req_q, all_k, all_v, valid)
    heads_out = jnp.concatenate(
        [prompt_out, req_out.reshape(REQ_DEV * QB, local_heads, HD)], axis=0
    )
    heads_out = heads_out.reshape(row_count, local_heads * HD)
    rows_dev = row_count // kv
    mixed = jnp.dot(heads_out, w_out, preferred_element_type=jnp.float32)
    mixed = mixed.reshape(kv, rows_dev, mixed.shape[1])

    def rows_of(part):
        return lax.dynamic_index_in_dim(mixed, part, 0, keepdims=False)

    own_rows = lax.dynamic_slice_in_dim(rows, me_kv * rows_dev, rows_dev, 0)
    resid = own_rows.astype(jnp.float32) + rows_of(me_kv)
    for turn in range(1, kv):
        sent = rows_of(lax.rem(me_kv + turn, kv)).astype(jnp.bfloat16)
        sent = lax.ppermute(sent, "kv", [(i, (i + turn) % kv) for i in range(kv)])
        resid = resid + sent.astype(jnp.float32)
    moe_in = rms_scale(resid, moe_gain).astype(jnp.bfloat16)
    moe_in, mine = lax.optimization_barrier((moe_in, mine))

    cores = 2
    order = chip_ring(ex // cores)
    chips = len(order)
    half = rows_dev // 2
    core = lax.rem(me, cores)
    ring, swap = [], [(i, i ^ 1) for i in range(ex)]
    table = np.zeros((ex, chips, 4), np.int32)
    for spot, chip in enumerate(order):
        for c in range(cores):
            here = chip * cores + c
            ring.append((here, order[(spot + 1 - 2 * c) % chips] * cores + c))
            for step in range(chips):
                own = order[(spot - step + 2 * c * step) % chips] * cores
                other = order[(spot + step - 2 * c * step) % chips] * cores
                table[here, step] = [
                    2 * (own + c) + c,
                    2 * (own + 1 - c) + c,
                    2 * (other + 1 - c) + 1 - c,
                    2 * (other + c) + 1 - c,
                ]
    places = lax.dynamic_index_in_dim(jnp.asarray(table), me, 0, keepdims=False)
    factor = jnp.take(factor.reshape(ex * 2, half), places.reshape(-1), axis=0)
    factor = factor.reshape(chips, 4 * half, 1)

    def half_of(array, which):
        return lax.dynamic_slice_in_dim(array, which * half, half, 0)

    got = lax.ppermute(half_of(moe_in, 1 - core), "ex", swap)
    held = jnp.concatenate([half_of(moe_in, core), got], axis=0)
    keeps, gots = [], []
    for step in range(chips):
        if step:
            held = lax.ppermute(held, "ex", ring)
        other = lax.ppermute(held, "ex", swap)
        keep, give = expert_ffn([held, other], factor[step], weights)
        keeps.append(keep)
        gots.append(lax.ppermute(give, "ex", swap))

    running = None
    for step in list(range(1, chips)) + [0]:
        term = keeps[step].astype(jnp.float32) + gots[step].astype(jnp.float32)
        if running is not None:
            term = term + running.astype(jnp.float32)
        running = term.astype(jnp.bfloat16)
        if step:
            running = lax.ppermute(running, "ex", ring)
    got = lax.ppermute(running[half:], "ex", swap)
    moe_out = jnp.where(
        core == 0,
        jnp.concatenate([running[:half], got], axis=0),
        jnp.concatenate([got, running[:half]], axis=0),
    )
    return (resid + moe_out.astype(jnp.float32)).astype(jnp.bfloat16)[None]


def solution(mesh):
    return jax.shard_map(
        on_device,
        mesh=mesh,
        in_specs=(
            P("ex", None, None),
            P(),
            P(None, None, "kv"),
            P("kv", None),
            P("ex", None, None, "kv"),
            P("ex"),
            P(),
            P(None, None, "ex", "kv"),
            P("ex", "kv", None),
            P("ex", "kv", None),
        ),
        out_specs=P("ex", "kv", None),
        check_vma=False,
    )
```

```python
import functools
import math

import jax
import jax.numpy as jnp
import numpy as np
from jax import lax
from jax.experimental import pallas as pl
from jax.experimental.pallas import tpu as pltpu
from jax.sharding import PartitionSpec as P

HD = 128
TOPK = 8
PLEN = 512
REQ_DEV = 2
QB = 32
CMAX = 512


def rms_scale(rows, gain):
    values = rows.astype(jnp.float32)
    scale = lax.rsqrt(jnp.mean(values * values, axis=-1, keepdims=True) + 1e-06)
    return values * scale * gain


def attention_kernel(scale, len_ref, x_ref, gain_ref, w_ref, cache_ref, w_out_ref, out_ref, normed):
    @pl.when(pl.program_id(0) == 0)
    def _():
        normed[...] = rms_scale(x_ref[...], gain_ref[...]).astype(jnp.bfloat16)
        out_ref[...] = jnp.zeros_like(out_ref)

    rows = normed[...]
    query, keys, values = (
        jnp.dot(rows, w_ref[j], preferred_element_type=jnp.float32).astype(jnp.bfloat16)
        for j in range(3)
    )

    def scores_of(q, k):
        return scale * lax.dot_general(
            q, k, (((1,), (1,)), ((), ())), preferred_element_type=jnp.float32
        )

    def mix(weights, v):
        return jnp.dot(weights.astype(jnp.bfloat16), v, preferred_element_type=jnp.float32)

    heads = []
    for head in range(query.shape[1] // HD):
        cut = slice(head * HD, (head + 1) * HD)
        q, k, v = query[:, cut], keys[:, cut], values[:, cut]
        scores = scores_of(q[:PLEN], k[:PLEN])
        weights = jnp.exp(scores - jnp.max(scores, axis=-1, keepdims=True))
        total = jnp.sum(weights, axis=-1, keepdims=True)
        outs = [(mix(weights, v[:PLEN]) / total).astype(jnp.bfloat16)]
        for request in range(REQ_DEV):
            own = slice(PLEN + request * QB, PLEN + (request + 1) * QB)
            fresh = scores_of(q[own], k[own])
            stored = scores_of(q[own], cache_ref[request, 0, :, cut])
            slots = lax.broadcasted_iota(jnp.int32, stored.shape, 1)
            stored = jnp.where(slots < len_ref[request], stored, -1e30)
            top = jnp.maximum(
                jnp.max(fresh, axis=-1, keepdims=True), jnp.max(stored, axis=-1, keepdims=True)
            )
            fresh, stored = jnp.exp(fresh - top), jnp.exp(stored - top)
            total = jnp.sum(fresh, axis=-1, keepdims=True) + jnp.sum(stored, axis=-1, keepdims=True)
            mixed = mix(fresh, v[own]) + mix(stored, cache_ref[request, 1, :, cut])
            outs.append((mixed / total).astype(jnp.bfloat16))
        heads.append(jnp.concatenate(outs, axis=0))
    out_ref[...] += jnp.dot(
        jnp.concatenate(heads, axis=1), w_out_ref[...], preferred_element_type=jnp.float32
    )


def attention(rows, gain, w_qkv, cache, cache_len, w_out):
    count, width = rows.shape
    units = w_qkv.shape[2]
    block = min(2 * HD, units)
    return pl.pallas_call(
        functools.partial(attention_kernel, 1.0 / math.sqrt(HD)),
        grid=(units // block,),
        in_specs=[
            pl.BlockSpec(memory_space=pltpu.SMEM),
            pl.BlockSpec((count, width), lambda i: (0, 0)),
            pl.BlockSpec((1, width), lambda i: (0, 0)),
            pl.BlockSpec((3, width, block), lambda i: (0, 0, i)),
            pl.BlockSpec((REQ_DEV, 2, CMAX, block), lambda i: (0, 0, 0, i)),
            pl.BlockSpec((block, width), lambda i: (i, 0)),
        ],
        out_specs=pl.BlockSpec((count, width), lambda i: (0, 0)),
        out_shape=jax.ShapeDtypeStruct((count, width), jnp.float32),
        scratch_shapes=[pltpu.VMEM((count, width), jnp.bfloat16)],
        compiler_params=pltpu.CompilerParams(vmem_limit_bytes=48 * 1024 * 1024),
        cost_estimate=pl.CostEstimate(
            flops=8 * count * width * units + 4 * PLEN * PLEN * units,
            bytes_accessed=8 * width * units + 6 * count * width,
            transcendentals=PLEN * PLEN * units // HD,
        ),
        name="attention",
    )(cache_len, rows, gain[None], jnp.transpose(w_qkv, (1, 0, 2)), cache, w_out)


def ffn_kernel(pieces, parts, refs):
    x_refs, share_ref = refs[:pieces], refs[pieces]
    weight_refs = refs[pieces + 1 : -4]
    keep_ref, give_ref, x_all, hidden = refs[-4:]
    width = x_all.shape[1]
    sources, slice_width, units = weight_refs[0].shape
    size, half = x_refs[0].shape[0], keep_ref.shape[0]
    for i in range(pieces):
        x_all[i * size : (i + 1) * size] = x_refs[i][...]

    block = min(256, units)
    for part in range(parts):

        def unit_step(i, carry):
            cut = pl.ds(pl.multiple_of(i * block, block), block)
            gate_w, up_w = (r[:, :, cut].reshape(width, block) for r in weight_refs[3 * part : 3 * part + 2])
            gate = jnp.dot(x_all[...], gate_w, preferred_element_type=jnp.float32)
            up = jnp.dot(x_all[...], up_w, preferred_element_type=jnp.float32)
            into = pl.ds(pl.multiple_of(part * units + i * block, block), block)
            hidden[:, into] = (gate * jax.nn.sigmoid(gate) * up).astype(jnp.bfloat16)
            return carry

        lax.fori_loop(0, units // block, unit_step, 0)

    group = max(1, min(sources, 512 // slice_width))
    columns = group * slice_width

    def width_step(i, carry):
        total = None
        for part in range(parts):
            down_w = weight_refs[3 * part + 2][pl.ds(i * group, group)].reshape(columns, units)
            term = lax.dot_general(
                hidden[:, part * units : (part + 1) * units],
                down_w,
                (((1,), (1,)), ((), ())),
                preferred_element_type=jnp.float32,
            )
            total = term if total is None else total + term
        total = (total * share_ref[...]).astype(jnp.bfloat16)
        cut = pl.ds(pl.multiple_of(i * columns, columns), columns)
        keep_ref[:, cut] = total[:half]
        give_ref[:, cut] = total[half:]
        return carry

    lax.fori_loop(0, sources // group, width_step, 0)


def expert_ffn(blocks, share, weights):
    half, width = blocks[0].shape
    if half % 16:
        blocks = [jnp.concatenate(blocks, axis=0)]
    pieces = len(blocks)
    count = 2 * half
    parts = len(weights) // 3
    hidden = parts * weights[0].shape[-1]
    vmem = pl.BlockSpec(memory_space=pltpu.VMEM)
    out = jax.ShapeDtypeStruct((half, width), jnp.bfloat16)
    return pl.pallas_call(
        lambda *refs: ffn_kernel(pieces, parts, refs),
        in_specs=[vmem] * (pieces + 1 + len(weights)),
        out_specs=[vmem] * 2,
        out_shape=[out, out],
        scratch_shapes=[
            pltpu.VMEM((count, width), jnp.bfloat16),
            pltpu.VMEM((count, hidden), jnp.bfloat16),
        ],
        compiler_params=pltpu.CompilerParams(vmem_limit_bytes=40 * 1024 * 1024),
        cost_estimate=pl.CostEstimate(
            flops=6 * count * width * hidden,
            bytes_accessed=4 * count * width + 6 * width * hidden,
            transcendentals=count * hidden,
        ),
        name="expert_ffn",
    )(*blocks, share, *weights)


def chip_ring(chips):
    rows = 4
    columns = chips // rows
    if chips % rows or columns < 2:
        return list(range(chips))
    order = [z * columns for z in range(rows)]
    for turn, z in enumerate(reversed(range(rows))):
        line = [z * columns + x for x in range(1, columns)]
        order += line if turn % 2 == 0 else line[::-1]
    return order


def on_device(
    x_tokens,
    attn_gain,
    w_qkv,
    w_out,
    cache,
    cache_len,
    moe_gain,
    w_trainer,
    expert_ids,
    route_probs,
):
    kv, ex = lax.axis_size("kv"), lax.axis_size("ex")
    me, me_kv = lax.axis_index("ex"), lax.axis_index("kv")
    experts = w_trainer.shape[0]

    def over_experts(kind):
        part = w_trainer[:, kind].astype(jnp.bfloat16)
        return lax.all_to_all(part, "ex", split_axis=0, concat_axis=0, tiled=True)

    def over_kv(part):
        return [
            lax.ppermute(part, "kv", [(i, (i + turn) % kv) for i in range(kv)])
            for turn in range(1, kv)
        ]

    probs = route_probs[0]
    share = probs / jnp.sum(probs, axis=-1, keepdims=True)
    named = expert_ids[0][:, :, None] == jnp.arange(experts, dtype=jnp.int32)[None, None, :]
    factor = jnp.sum(jnp.where(named, share[:, :, None], 0.0), axis=1)
    factor = lax.all_gather(factor, "ex", axis=0)
    factor = jnp.sum(jnp.where(jnp.arange(experts) == me, factor, 0.0), axis=-1)

    rows = x_tokens[0]
    row_count = rows.shape[0]
    rows_dev = row_count // kv
    gate = over_experts(0)
    mixed = attention(rows, attn_gain, w_qkv, cache, cache_len, w_out)
    mixed, gate = lax.optimization_barrier((mixed, gate))
    gates = over_kv(gate)
    up = over_experts(1)
    mixed = mixed.reshape(kv, rows_dev, mixed.shape[1])

    def rows_of(part):
        return lax.dynamic_index_in_dim(mixed, part, 0, keepdims=False)

    own_rows = lax.dynamic_slice_in_dim(rows, me_kv * rows_dev, rows_dev, 0)
    resid = own_rows.astype(jnp.float32) + rows_of(me_kv)
    for turn in range(1, kv):
        sent = rows_of(lax.rem(me_kv + turn, kv)).astype(jnp.bfloat16)
        sent = lax.ppermute(sent, "kv", [(i, (i + turn) % kv) for i in range(kv)])
        resid = resid + sent.astype(jnp.float32)
    moe_in = rms_scale(resid, moe_gain).astype(jnp.bfloat16)
    moe_in, gates, up, factor = lax.optimization_barrier((moe_in, gates, up, factor))
    ups = over_kv(up)
    down = over_experts(2)

    cores = 2
    order = chip_ring(ex // cores)
    chips = len(order)
    half = rows_dev // 2
    core = lax.rem(me, cores)
    ring, swap = [], [(i, i ^ 1) for i in range(ex)]
    table = np.zeros((ex, chips, 4), np.int32)
    for spot, chip in enumerate(order):
        for c in range(cores):
            here = chip * cores + c
            ring.append((here, order[(spot + 1 - 2 * c) % chips] * cores + c))
            for step in range(chips):
                own = order[(spot - step + 2 * c * step) % chips] * cores
                other = order[(spot + step - 2 * c * step) % chips] * cores
                table[here, step] = [
                    2 * (own + c) + c,
                    2 * (own + 1 - c) + c,
                    2 * (other + 1 - c) + 1 - c,
                    2 * (other + c) + 1 - c,
                ]
    places = lax.dynamic_index_in_dim(jnp.asarray(table), me, 0, keepdims=False)
    factor = jnp.take(factor.reshape(ex * 2, half), places.reshape(-1), axis=0)
    factor = factor.reshape(chips, 4 * half, 1)

    def half_of(array, which):
        return lax.dynamic_slice_in_dim(array, which * half, half, 0)

    got = lax.ppermute(half_of(moe_in, 1 - core), "ex", swap)
    held = jnp.concatenate([half_of(moe_in, core), got], axis=0)
    ahead = min(5, chips - 1)
    held = [held]
    for step in range(1, chips):
        held.append(lax.ppermute(held[-1], "ex", ring))
        if step == min(2, ahead):
            held[-1], ups, down = lax.optimization_barrier((held[-1], ups, down))
            downs = over_kv(down)
        if step == ahead:
            held[-1], gate = lax.optimization_barrier((held[-1], gate))
    weights = [gate, up, down]
    for turn in range(kv - 1):
        weights += [gates[turn], ups[turn], downs[turn]]

    keeps, gots = [], []
    for step in range(chips):
        other = lax.ppermute(held[step], "ex", swap)
        keep, give = expert_ffn([held[step], other], factor[step], weights)
        keeps.append(keep)
        gots.append(lax.ppermute(give, "ex", swap))

    running = None
    for step in list(range(1, chips)) + [0]:
        term = keeps[step].astype(jnp.float32) + gots[step].astype(jnp.float32)
        if running is not None:
            term = term + running.astype(jnp.float32)
        running = term.astype(jnp.bfloat16)
        if step:
            running = lax.ppermute(running, "ex", ring)
    got = lax.ppermute(running[half:], "ex", swap)
    moe_out = jnp.where(
        core == 0,
        jnp.concatenate([running[:half], got], axis=0),
        jnp.concatenate([got, running[:half]], axis=0),
    )
    return (resid + moe_out.astype(jnp.float32)).astype(jnp.bfloat16)[None]


def solution(mesh):
    return jax.shard_map(
        on_device,
        mesh=mesh,
        in_specs=(
            P("ex", None, None),
            P(),
            P(None, None, "kv"),
            P("kv", None),
            P("ex", None, None, "kv"),
            P("ex"),
            P(),
            P(None, None, "ex", "kv"),
            P("ex", "kv", None),
            P("ex", "kv", None),
        ),
        out_specs=P("ex", "kv", None),
        check_vma=False,
    )
```

```python
import functools
import math

import jax
import jax.numpy as jnp
import numpy as np
from jax import lax
from jax.experimental import pallas as pl
from jax.experimental.pallas import tpu as pltpu
from jax.sharding import PartitionSpec as P

HD = 128
TOPK = 8
PLEN = 512
REQ_DEV = 2
QB = 32
CMAX = 512


def rms_scale(rows, gain):
    values = rows.astype(jnp.float32)
    scale = lax.rsqrt(jnp.mean(values * values, axis=-1, keepdims=True) + 1e-06)
    return values * scale * gain


def attention_kernel(scale, len_ref, x_ref, gain_ref, w_ref, cache_ref, w_out_ref, out_ref, normed):
    @pl.when(pl.program_id(0) == 0)
    def _():
        normed[...] = rms_scale(x_ref[...], gain_ref[...]).astype(jnp.bfloat16)
        out_ref[...] = jnp.zeros_like(out_ref)

    rows = normed[...]
    query, keys, values = (
        jnp.dot(rows, w_ref[j], preferred_element_type=jnp.float32).astype(jnp.bfloat16)
        for j in range(3)
    )

    def scores_of(q, k):
        return scale * lax.dot_general(
            q, k, (((1,), (1,)), ((), ())), preferred_element_type=jnp.float32
        )

    def mix(weights, v):
        return jnp.dot(weights.astype(jnp.bfloat16), v, preferred_element_type=jnp.float32)

    heads = []
    for head in range(query.shape[1] // HD):
        cut = slice(head * HD, (head + 1) * HD)
        q, k, v = query[:, cut], keys[:, cut], values[:, cut]
        scores = scores_of(q[:PLEN], k[:PLEN])
        weights = jnp.exp(scores - jnp.max(scores, axis=-1, keepdims=True))
        total = jnp.sum(weights, axis=-1, keepdims=True)
        outs = [(mix(weights, v[:PLEN]) / total).astype(jnp.bfloat16)]
        for request in range(REQ_DEV):
            own = slice(PLEN + request * QB, PLEN + (request + 1) * QB)
            fresh = scores_of(q[own], k[own])
            stored = scores_of(q[own], cache_ref[request, 0, :, cut])
            slots = lax.broadcasted_iota(jnp.int32, stored.shape, 1)
            stored = jnp.where(slots < len_ref[request], stored, -1e30)
            top = jnp.maximum(
                jnp.max(fresh, axis=-1, keepdims=True), jnp.max(stored, axis=-1, keepdims=True)
            )
            fresh, stored = jnp.exp(fresh - top), jnp.exp(stored - top)
            total = jnp.sum(fresh, axis=-1, keepdims=True) + jnp.sum(stored, axis=-1, keepdims=True)
            mixed = mix(fresh, v[own]) + mix(stored, cache_ref[request, 1, :, cut])
            outs.append((mixed / total).astype(jnp.bfloat16))
        heads.append(jnp.concatenate(outs, axis=0))
    out_ref[...] += jnp.dot(
        jnp.concatenate(heads, axis=1), w_out_ref[...], preferred_element_type=jnp.float32
    )


def attention(rows, gain, w_qkv, cache, cache_len, w_out):
    count, width = rows.shape
    units = w_qkv.shape[2]
    block = min(2 * HD, units)
    return pl.pallas_call(
        functools.partial(attention_kernel, 1.0 / math.sqrt(HD)),
        grid=(units // block,),
        in_specs=[
            pl.BlockSpec(memory_space=pltpu.SMEM),
            pl.BlockSpec((count, width), lambda i: (0, 0)),
            pl.BlockSpec((1, width), lambda i: (0, 0)),
            pl.BlockSpec((3, width, block), lambda i: (0, 0, i)),
            pl.BlockSpec((REQ_DEV, 2, CMAX, block), lambda i: (0, 0, 0, i)),
            pl.BlockSpec((block, width), lambda i: (i, 0)),
        ],
        out_specs=pl.BlockSpec((count, width), lambda i: (0, 0)),
        out_shape=jax.ShapeDtypeStruct((count, width), jnp.float32),
        scratch_shapes=[pltpu.VMEM((count, width), jnp.bfloat16)],
        compiler_params=pltpu.CompilerParams(vmem_limit_bytes=48 * 1024 * 1024),
        cost_estimate=pl.CostEstimate(
            flops=8 * count * width * units + 4 * PLEN * PLEN * units,
            bytes_accessed=8 * width * units + 6 * count * width,
            transcendentals=PLEN * PLEN * units // HD,
        ),
        name="attention",
    )(cache_len, rows, gain[None], jnp.transpose(w_qkv, (1, 0, 2)), cache, w_out)


def ffn_kernel(pieces, parts, refs):
    x_refs, share_ref = refs[:pieces], refs[pieces]
    weight_refs = refs[pieces + 1 : -4]
    keep_ref, give_ref, x_all, hidden = refs[-4:]
    width = x_all.shape[1]
    sources, slice_width, units = weight_refs[0].shape
    size, half = x_refs[0].shape[0], keep_ref.shape[0]
    for i in range(pieces):
        x_all[i * size : (i + 1) * size] = x_refs[i][...]

    for part in range(parts):
        gate_w, up_w = (r[...].reshape(width, units) for r in weight_refs[3 * part : 3 * part + 2])
        gate = jnp.dot(x_all[...], gate_w, preferred_element_type=jnp.float32)
        up = jnp.dot(x_all[...], up_w, preferred_element_type=jnp.float32)
        hidden[:, part * units : (part + 1) * units] = (gate * jax.nn.sigmoid(gate) * up).astype(
            jnp.bfloat16
        )

    group = max(1, min(sources, 1024 // slice_width))
    for first in range(0, sources, group):
        total = None
        for part in range(parts):
            down_w = weight_refs[3 * part + 2][first : first + group]
            term = lax.dot_general(
                hidden[:, part * units : (part + 1) * units],
                down_w.reshape(group * slice_width, units),
                (((1,), (1,)), ((), ())),
                preferred_element_type=jnp.float32,
            )
            total = term if total is None else total + term
        total = (total * share_ref[...]).astype(jnp.bfloat16)
        cut = slice(first * slice_width, (first + group) * slice_width)
        keep_ref[:, cut] = total[:half]
        give_ref[:, cut] = total[half:]


def expert_ffn(blocks, share, weights):
    half, width = blocks[0].shape
    if half % 16:
        blocks = [jnp.concatenate(blocks, axis=0)]
    pieces = len(blocks)
    count = 2 * half
    parts = len(weights) // 3
    hidden = parts * weights[0].shape[-1]
    vmem = pl.BlockSpec(memory_space=pltpu.VMEM)
    out = jax.ShapeDtypeStruct((half, width), jnp.bfloat16)
    return pl.pallas_call(
        lambda *refs: ffn_kernel(pieces, parts, refs),
        in_specs=[vmem] * (pieces + 1 + len(weights)),
        out_specs=[vmem] * 2,
        out_shape=[out, out],
        scratch_shapes=[
            pltpu.VMEM((count, width), jnp.bfloat16),
            pltpu.VMEM((count, hidden), jnp.bfloat16),
        ],
        compiler_params=pltpu.CompilerParams(vmem_limit_bytes=20 * 1024 * 1024),
        cost_estimate=pl.CostEstimate(
            flops=6 * count * width * hidden,
            bytes_accessed=4 * count * width + 6 * width * hidden,
            transcendentals=count * hidden,
        ),
        name="expert_ffn",
    )(*blocks, share, *weights)


def sum_kernel(cut, refs):
    total = refs[0][:, cut].astype(jnp.float32) + refs[1][:, cut].astype(jnp.float32)
    for ref in refs[2:-1]:
        total = total + ref[...].astype(jnp.float32)
    refs[-1][...] = total.astype(jnp.bfloat16)


def add_terms(cut, keep, got, running):
    terms = [keep, got] + ([] if running is None else [running])
    columns = cut.stop - cut.start
    vmem = pl.BlockSpec(memory_space=pltpu.VMEM)
    return pl.pallas_call(
        lambda *refs: sum_kernel(cut, refs),
        in_specs=[vmem] * len(terms),
        out_specs=vmem,
        out_shape=jax.ShapeDtypeStruct((keep.shape[0], columns), jnp.bfloat16),
        compiler_params=pltpu.CompilerParams(vmem_limit_bytes=16 * 1024 * 1024),
        cost_estimate=pl.CostEstimate(
            flops=2 * keep.shape[0] * columns,
            bytes_accessed=8 * keep.shape[0] * columns,
            transcendentals=0,
        ),
        name="add_terms",
    )(*terms)


def chip_ring(chips):
    rows = 4
    columns = chips // rows
    if chips % rows or columns < 2:
        return list(range(chips))
    order = [z * columns for z in range(rows)]
    for turn, z in enumerate(reversed(range(rows))):
        line = [z * columns + x for x in range(1, columns)]
        order += line if turn % 2 == 0 else line[::-1]
    return order


def on_device(
    x_tokens,
    attn_gain,
    w_qkv,
    w_out,
    cache,
    cache_len,
    moe_gain,
    w_trainer,
    expert_ids,
    route_probs,
):
    kv, ex = lax.axis_size("kv"), lax.axis_size("ex")
    me, me_kv = lax.axis_index("ex"), lax.axis_index("kv")
    experts = w_trainer.shape[0]

    def over_experts(part):
        return lax.all_to_all(part, "ex", split_axis=0, concat_axis=0, tiled=True)

    def over_kv(part):
        return [
            lax.ppermute(part, "kv", [(i, (i + turn) % kv) for i in range(kv)])
            for turn in range(1, kv)
        ]

    probs = route_probs[0]
    share = probs / jnp.sum(probs, axis=-1, keepdims=True)
    named = expert_ids[0][:, :, None] == jnp.arange(experts, dtype=jnp.int32)[None, None, :]
    factor = jnp.sum(jnp.where(named, share[:, :, None], 0.0), axis=1)
    factor = lax.all_gather(factor, "ex", axis=0)
    factor = jnp.sum(jnp.where(jnp.arange(experts) == me, factor, 0.0), axis=-1)

    rows = x_tokens[0]
    row_count = rows.shape[0]
    rows_dev = row_count // kv
    gate, up, down = (w_trainer[:, kind].astype(jnp.bfloat16) for kind in range(3))
    gate = over_experts(gate)
    mixed = attention(rows, attn_gain, w_qkv, cache, cache_len, w_out)
    mixed, gate, up, down = lax.optimization_barrier((mixed, gate, up, down))
    gates = over_kv(gate)
    up = over_experts(up)
    mixed = mixed.reshape(kv, rows_dev, mixed.shape[1])

    def rows_of(part):
        return lax.dynamic_index_in_dim(mixed, part, 0, keepdims=False)

    own_rows = lax.dynamic_slice_in_dim(rows, me_kv * rows_dev, rows_dev, 0)
    resid = own_rows.astype(jnp.float32) + rows_of(me_kv)
    for turn in range(1, kv):
        sent = rows_of(lax.rem(me_kv + turn, kv)).astype(jnp.bfloat16)
        sent = lax.ppermute(sent, "kv", [(i, (i + turn) % kv) for i in range(kv)])
        resid = resid + sent.astype(jnp.float32)
    moe_in = rms_scale(resid, moe_gain).astype(jnp.bfloat16)
    moe_in, up, down, factor = lax.optimization_barrier((moe_in, up, down, factor))
    ups = over_kv(up)
    down = over_experts(down)

    cores = 2
    order = chip_ring(ex // cores)
    chips = len(order)
    half = rows_dev // 2
    core = lax.rem(me, cores)
    ring, swap = [], [(i, i ^ 1) for i in range(ex)]
    table = np.zeros((ex, chips, 4), np.int32)
    for spot, chip in enumerate(order):
        for c in range(cores):
            here = chip * cores + c
            ring.append((here, order[(spot + 1 - 2 * c) % chips] * cores + c))
            for step in range(chips):
                own = order[(spot - step + 2 * c * step) % chips] * cores
                other = order[(spot + step - 2 * c * step) % chips] * cores
                table[here, step] = [
                    2 * (own + c) + c,
                    2 * (own + 1 - c) + c,
                    2 * (other + 1 - c) + 1 - c,
                    2 * (other + c) + 1 - c,
                ]
    places = lax.dynamic_index_in_dim(jnp.asarray(table), me, 0, keepdims=False)
    factor = jnp.take(factor.reshape(ex * 2, half), places.reshape(-1), axis=0)
    factor = factor.reshape(chips, 4 * half, 1)

    def half_of(array, which):
        return lax.dynamic_slice_in_dim(array, which * half, half, 0)

    got = lax.ppermute(half_of(moe_in, 1 - core), "ex", swap)
    held = jnp.concatenate([half_of(moe_in, core), got], axis=0)
    ahead = min(5, chips - 1)
    held = [held]
    for step in range(1, chips):
        held.append(lax.ppermute(held[-1], "ex", ring))
        if step == min(2, ahead):
            held[-1], gates, down = lax.optimization_barrier((held[-1], gates, down))
            downs = over_kv(down)
        if step == ahead:
            held[-1], gate, ups = lax.optimization_barrier((held[-1], gate, ups))
    weights = [gate, up, down]
    for turn in range(kv - 1):
        weights += [gates[turn], ups[turn], downs[turn]]

    keeps, gots = [], []
    for step in range(chips):
        other = lax.ppermute(held[step], "ex", swap)
        keep, give = expert_ffn([held[step], other], factor[step], weights)
        keeps.append(keep)
        gots.append(lax.ppermute(give, "ex", swap))

    width = moe_in.shape[1]
    sums = []
    for cut in (slice(0, width // 2), slice(width // 2, width)):
        running = None
        for step in list(range(1, chips)) + [0]:
            running = add_terms(cut, keeps[step], gots[step], running)
            if step:
                running = lax.ppermute(running, "ex", ring)
        sums.append(running)
    running = jnp.concatenate(sums, axis=1)
    got = lax.ppermute(running[half:], "ex", swap)
    moe_out = jnp.where(
        core == 0,
        jnp.concatenate([running[:half], got], axis=0),
        jnp.concatenate([got, running[:half]], axis=0),
    )
    return (resid + moe_out.astype(jnp.float32)).astype(jnp.bfloat16)[None]


def solution(mesh):
    return jax.shard_map(
        on_device,
        mesh=mesh,
        in_specs=(
            P("ex", None, None),
            P(),
            P(None, None, "kv"),
            P("kv", None),
            P("ex", None, None, "kv"),
            P("ex"),
            P(),
            P(None, None, "ex", "kv"),
            P("ex", "kv", None),
            P("ex", "kv", None),
        ),
        out_specs=P("ex", "kv", None),
        check_vma=False,
    )
```

```python
import functools
import math

import jax
import jax.numpy as jnp
from jax import lax
from jax.experimental import pallas as pl
from jax.experimental.pallas import tpu as pltpu
from jax.sharding import PartitionSpec as P

HD = 128
TOPK = 8
PLEN = 512
REQ_DEV = 2
QB = 32
CMAX = 512


def rms_scale(rows, gain):
    values = rows.astype(jnp.float32)
    scale = lax.rsqrt(jnp.mean(values * values, axis=-1, keepdims=True) + 1e-06)
    return values * scale * gain


def attention_kernel(scale, len_ref, x_ref, gain_ref, w_ref, cache_ref, w_out_ref, out_ref, normed):
    @pl.when(pl.program_id(0) == 0)
    def _():
        normed[...] = rms_scale(x_ref[...], gain_ref[...]).astype(jnp.bfloat16)
        out_ref[...] = jnp.zeros_like(out_ref)

    rows = normed[...]
    query, keys, values = (
        jnp.dot(rows, w_ref[j], preferred_element_type=jnp.float32).astype(jnp.bfloat16)
        for j in range(3)
    )

    def scores_of(q, k):
        return scale * lax.dot_general(
            q, k, (((1,), (1,)), ((), ())), preferred_element_type=jnp.float32
        )

    def mix(weights, v):
        return jnp.dot(weights.astype(jnp.bfloat16), v, preferred_element_type=jnp.float32)

    heads = []
    for head in range(query.shape[1] // HD):
        cut = slice(head * HD, (head + 1) * HD)
        q, k, v = query[:, cut], keys[:, cut], values[:, cut]
        scores = scores_of(q[:PLEN], k[:PLEN])
        weights = jnp.exp(scores - jnp.max(scores, axis=-1, keepdims=True))
        total = jnp.sum(weights, axis=-1, keepdims=True)
        outs = [(mix(weights, v[:PLEN]) / total).astype(jnp.bfloat16)]
        for request in range(REQ_DEV):
            own = slice(PLEN + request * QB, PLEN + (request + 1) * QB)
            fresh = scores_of(q[own], k[own])
            stored = scores_of(q[own], cache_ref[request, 0, :, cut])
            slots = lax.broadcasted_iota(jnp.int32, stored.shape, 1)
            stored = jnp.where(slots < len_ref[request], stored, -1e30)
            top = jnp.maximum(
                jnp.max(fresh, axis=-1, keepdims=True), jnp.max(stored, axis=-1, keepdims=True)
            )
            fresh, stored = jnp.exp(fresh - top), jnp.exp(stored - top)
            total = jnp.sum(fresh, axis=-1, keepdims=True) + jnp.sum(stored, axis=-1, keepdims=True)
            mixed = mix(fresh, v[own]) + mix(stored, cache_ref[request, 1, :, cut])
            outs.append((mixed / total).astype(jnp.bfloat16))
        heads.append(jnp.concatenate(outs, axis=0))
    out_ref[...] += jnp.dot(
        jnp.concatenate(heads, axis=1), w_out_ref[...], preferred_element_type=jnp.float32
    )


def attention(rows, gain, w_qkv, cache, cache_len, w_out):
    count, width = rows.shape
    units = w_qkv.shape[2]
    block = min(2 * HD, units)
    return pl.pallas_call(
        functools.partial(attention_kernel, 1.0 / math.sqrt(HD)),
        grid=(units // block,),
        in_specs=[
            pl.BlockSpec(memory_space=pltpu.SMEM),
            pl.BlockSpec((count, width), lambda i: (0, 0)),
            pl.BlockSpec((1, width), lambda i: (0, 0)),
            pl.BlockSpec((3, width, block), lambda i: (0, 0, i)),
            pl.BlockSpec((REQ_DEV, 2, CMAX, block), lambda i: (0, 0, 0, i)),
            pl.BlockSpec((block, width), lambda i: (i, 0)),
        ],
        out_specs=pl.BlockSpec((count, width), lambda i: (0, 0)),
        out_shape=jax.ShapeDtypeStruct((count, width), jnp.float32),
        scratch_shapes=[pltpu.VMEM((count, width), jnp.bfloat16)],
        compiler_params=pltpu.CompilerParams(vmem_limit_bytes=48 * 1024 * 1024),
        cost_estimate=pl.CostEstimate(
            flops=8 * count * width * units + 4 * PLEN * PLEN * units,
            bytes_accessed=8 * width * units + 6 * count * width,
            transcendentals=PLEN * PLEN * units // HD,
        ),
        name="attention",
    )(cache_len, rows, gain[None], jnp.transpose(w_qkv, (1, 0, 2)), cache, w_out)


def share_columns(share):
    high = share.astype(jnp.bfloat16)
    low = (share - high.astype(jnp.float32)).astype(jnp.bfloat16)
    spare = -2 * share.shape[1] % 128
    return jnp.concatenate([high, low, jnp.zeros((share.shape[0], spare), jnp.bfloat16)], axis=1)


def hidden_kernel(experts, width, me_ref, *refs):
    x_refs, weight_refs, out_refs = refs[:2], refs[2:-2], refs[-2:]
    units = weight_refs[0].shape[2]
    me = me_ref[0]
    for x_ref, out_ref in zip(x_refs, out_refs):
        extra = x_ref[:, width:].astype(jnp.float32)
        lanes = lax.broadcasted_iota(jnp.int32, extra.shape, 1)
        mine = (lanes == me) | (lanes == me + experts)
        share = jnp.sum(jnp.where(mine, extra, 0.0), axis=-1, keepdims=True)
        for part in range(len(weight_refs) // 2):
            gate_w, up_w = (r[...].reshape(width, units) for r in weight_refs[2 * part : 2 * part + 2])
            x = x_ref[:, :width]
            gate = jnp.dot(x, gate_w, preferred_element_type=jnp.float32)
            up = jnp.dot(x, up_w, preferred_element_type=jnp.float32)
            out_ref[:, part * units : (part + 1) * units] = (
                gate * jax.nn.sigmoid(gate) * up * share
            ).astype(jnp.bfloat16)


def expert_hidden(experts, me, blocks, weights):
    count = blocks[0].shape[0]
    sources, slice_width, units = weights[0].shape
    width, hidden = sources * slice_width, units * len(weights) // 2
    vmem = pl.BlockSpec(memory_space=pltpu.VMEM)
    out = jax.ShapeDtypeStruct((count, hidden), jnp.bfloat16)
    return pl.pallas_call(
        functools.partial(hidden_kernel, experts, width),
        in_specs=[pl.BlockSpec(memory_space=pltpu.SMEM)] + [vmem] * (2 + len(weights)),
        out_specs=[vmem] * 2,
        out_shape=[out, out],
        compiler_params=pltpu.CompilerParams(vmem_limit_bytes=16 * 1024 * 1024),
        cost_estimate=pl.CostEstimate(
            flops=8 * count * width * hidden,
            bytes_accessed=4 * count * (width + hidden) + 4 * width * hidden,
            transcendentals=2 * count * hidden,
        ),
        name="expert_hidden",
    )(me, *blocks, *weights)


def down_kernel(*refs):
    hidden_refs, weight_refs, out_refs = refs[:2], refs[2:-2], refs[-2:]
    sources, slice_width, units = weight_refs[0].shape
    group = max(1, min(sources, 1024 // slice_width))
    for hidden_ref, out_ref in zip(hidden_refs, out_refs):
        for first in range(0, sources, group):
            total = None
            for part, weight_ref in enumerate(weight_refs):
                term = lax.dot_general(
                    hidden_ref[:, part * units : (part + 1) * units],
                    weight_ref[first : first + group].reshape(group * slice_width, units),
                    (((1,), (1,)), ((), ())),
                    preferred_element_type=jnp.float32,
                )
                total = term if total is None else total + term
            cut = slice(first * slice_width, (first + group) * slice_width)
            out_ref[:, cut] = total.astype(jnp.bfloat16)


def expert_down(hiddens, weights):
    count, hidden = hiddens[0].shape
    width = weights[0].shape[0] * weights[0].shape[1]
    vmem = pl.BlockSpec(memory_space=pltpu.VMEM)
    out = jax.ShapeDtypeStruct((count, width), jnp.bfloat16)
    return pl.pallas_call(
        down_kernel,
        in_specs=[vmem] * (2 + len(weights)),
        out_specs=[vmem] * 2,
        out_shape=[out, out],
        compiler_params=pltpu.CompilerParams(vmem_limit_bytes=16 * 1024 * 1024),
        cost_estimate=pl.CostEstimate(
            flops=4 * count * width * hidden,
            bytes_accessed=4 * count * (width + hidden) + 2 * width * hidden,
            transcendentals=0,
        ),
        name="expert_down",
    )(*hiddens, *weights)


def sum_kernel(cut, refs):
    total = refs[0][:, cut].astype(jnp.float32) + refs[1][:, cut].astype(jnp.float32)
    for ref in refs[2:-1]:
        total = total + ref[...].astype(jnp.float32)
    refs[-1][...] = total.astype(jnp.bfloat16)


def add_terms(cut, keep, got, running):
    terms = [keep, got] + ([] if running is None else [running])
    columns = cut.stop - cut.start
    vmem = pl.BlockSpec(memory_space=pltpu.VMEM)
    return pl.pallas_call(
        lambda *refs: sum_kernel(cut, refs),
        in_specs=[vmem] * len(terms),
        out_specs=vmem,
        out_shape=jax.ShapeDtypeStruct((keep.shape[0], columns), jnp.bfloat16),
        compiler_params=pltpu.CompilerParams(vmem_limit_bytes=16 * 1024 * 1024),
        cost_estimate=pl.CostEstimate(
            flops=2 * keep.shape[0] * columns,
            bytes_accessed=8 * keep.shape[0] * columns,
            transcendentals=0,
        ),
        name="add_terms",
    )(*terms)


def chip_ring(chips):
    rows = 4
    columns = chips // rows
    if chips % rows or columns < 2:
        return list(range(chips))
    order = [z * columns for z in range(rows)]
    for turn, z in enumerate(reversed(range(rows))):
        line = [z * columns + x for x in range(1, columns)]
        order += line if turn % 2 == 0 else line[::-1]
    return order


def on_device(
    x_tokens,
    attn_gain,
    w_qkv,
    w_out,
    cache,
    cache_len,
    moe_gain,
    w_trainer,
    expert_ids,
    route_probs,
):
    kv, ex = lax.axis_size("kv"), lax.axis_size("ex")
    me, me_kv = lax.axis_index("ex"), lax.axis_index("kv")
    experts = w_trainer.shape[0]

    def over_experts(part):
        return lax.all_to_all(part, "ex", split_axis=0, concat_axis=0, tiled=True)

    def over_kv(part):
        return [
            lax.ppermute(part, "kv", [(i, (i + turn) % kv) for i in range(kv)])
            for turn in range(1, kv)
        ]

    probs = route_probs[0]
    share = probs / jnp.sum(probs, axis=-1, keepdims=True)
    named = expert_ids[0][:, :, None] == jnp.arange(experts, dtype=jnp.int32)[None, None, :]
    factor = jnp.sum(jnp.where(named, share[:, :, None], 0.0), axis=1)
    factor = share_columns(factor)

    rows = x_tokens[0]
    row_count = rows.shape[0]
    rows_dev = row_count // kv
    gate, up, down = (w_trainer[:, kind].astype(jnp.bfloat16) for kind in range(3))
    gate = over_experts(gate)
    mixed = attention(rows, attn_gain, w_qkv, cache, cache_len, w_out)
    mixed, gate, up, down = lax.optimization_barrier((mixed, gate, up, down))
    gates = over_kv(gate)
    up = over_experts(up)
    mixed = mixed.reshape(kv, rows_dev, mixed.shape[1])

    def rows_of(part):
        return lax.dynamic_index_in_dim(mixed, part, 0, keepdims=False)

    own_rows = lax.dynamic_slice_in_dim(rows, me_kv * rows_dev, rows_dev, 0)
    resid = own_rows.astype(jnp.float32) + rows_of(me_kv)
    for turn in range(1, kv):
        sent = rows_of(lax.rem(me_kv + turn, kv)).astype(jnp.bfloat16)
        sent = lax.ppermute(sent, "kv", [(i, (i + turn) % kv) for i in range(kv)])
        resid = resid + sent.astype(jnp.float32)
    moe_in = rms_scale(resid, moe_gain).astype(jnp.bfloat16)
    moe_in = jnp.concatenate([moe_in, factor], axis=1)
    moe_in, gates, up, down = lax.optimization_barrier((moe_in, gates, up, down))
    ups = over_kv(up)
    down = over_experts(down)

    cores = 2
    order = chip_ring(ex // cores)
    chips = len(order)
    half = rows_dev // 2
    core = lax.rem(me, cores)
    ring, swap = [], [(i, i ^ 1) for i in range(ex)]
    for spot, chip in enumerate(order):
        for c in range(cores):
            here = chip * cores + c
            ring.append((here, order[(spot + 1 - 2 * c) % chips] * cores + c))

    def half_of(array, which):
        return lax.dynamic_slice_in_dim(array, which * half, half, 0)

    got = lax.ppermute(half_of(moe_in, 1 - core), "ex", swap)
    held = jnp.concatenate([half_of(moe_in, core), got], axis=0)
    blocks = [held]
    for step in range(1, chips):
        held = lax.ppermute(held, "ex", ring)
        if step == min(2, chips - 1):
            held, ups, down = lax.optimization_barrier((held, ups, down))
            downs = over_kv(down)
        blocks.append(held)

    first_weights = [gate, up]
    for turn in range(kv - 1):
        first_weights += [gates[turn], ups[turn]]
    hiddens = []
    for block in blocks:
        other = lax.ppermute(block, "ex", swap)
        hiddens.append(expert_hidden(experts, me[None], [block, other], first_weights))
    ahead = chips
    hiddens[:ahead], downs = lax.optimization_barrier((hiddens[:ahead], downs))
    keeps, gots = [], []
    for pair in hiddens:
        keep, give = expert_down(pair, [down] + downs)
        keeps.append(keep)
        gots.append(lax.ppermute(give, "ex", swap))

    width = w_out.shape[1]
    sums = []
    for cut in (slice(0, width // 2), slice(width // 2, width)):
        running = None
        for step in list(range(1, chips)) + [0]:
            running = add_terms(cut, keeps[step], gots[step], running)
            if step:
                running = lax.ppermute(running, "ex", ring)
        sums.append(running)
    running = jnp.concatenate(sums, axis=1)
    got = lax.ppermute(running[half:], "ex", swap)
    moe_out = jnp.where(
        core == 0,
        jnp.concatenate([running[:half], got], axis=0),
        jnp.concatenate([got, running[:half]], axis=0),
    )
    return (resid + moe_out.astype(jnp.float32)).astype(jnp.bfloat16)[None]


def solution(mesh):
    return jax.shard_map(
        on_device,
        mesh=mesh,
        in_specs=(
            P("ex", None, None),
            P(),
            P(None, None, "kv"),
            P("kv", None),
            P("ex", None, None, "kv"),
            P("ex"),
            P(),
            P(None, None, "ex", "kv"),
            P("ex", "kv", None),
            P("ex", "kv", None),
        ),
        out_specs=P("ex", "kv", None),
        check_vma=False,
    )
```

```python
import functools
import math

import jax
import jax.numpy as jnp
from jax import lax
from jax.experimental import pallas as pl
from jax.experimental.pallas import tpu as pltpu
from jax.sharding import PartitionSpec as P

HD = 128
TOPK = 8
PLEN = 512
REQ_DEV = 2
QB = 32
CMAX = 512


def rms_scale(rows, gain):
    values = rows.astype(jnp.float32)
    scale = lax.rsqrt(jnp.mean(values * values, axis=-1, keepdims=True) + 1e-06)
    return values * scale * gain


def attention_kernel(scale, len_ref, x_ref, gain_ref, w_ref, cache_ref, w_out_ref, out_ref, normed):
    @pl.when(pl.program_id(0) == 0)
    def _():
        normed[...] = rms_scale(x_ref[...], gain_ref[...]).astype(jnp.bfloat16)
        out_ref[...] = jnp.zeros_like(out_ref)

    rows = normed[...]
    query, keys, values = (
        jnp.dot(rows, w_ref[j], preferred_element_type=jnp.float32).astype(jnp.bfloat16)
        for j in range(3)
    )

    def scores_of(q, k):
        return scale * lax.dot_general(
            q, k, (((1,), (1,)), ((), ())), preferred_element_type=jnp.float32
        )

    def mix(weights, v):
        return jnp.dot(weights.astype(jnp.bfloat16), v, preferred_element_type=jnp.float32)

    heads = []
    for head in range(query.shape[1] // HD):
        cut = slice(head * HD, (head + 1) * HD)
        q, k, v = query[:, cut], keys[:, cut], values[:, cut]
        scores = scores_of(q[:PLEN], k[:PLEN])
        weights = jnp.exp(scores - jnp.max(scores, axis=-1, keepdims=True))
        total = jnp.sum(weights, axis=-1, keepdims=True)
        outs = [(mix(weights, v[:PLEN]) / total).astype(jnp.bfloat16)]
        for request in range(REQ_DEV):
            own = slice(PLEN + request * QB, PLEN + (request + 1) * QB)
            fresh = scores_of(q[own], k[own])
            stored = scores_of(q[own], cache_ref[request, 0, :, cut])
            slots = lax.broadcasted_iota(jnp.int32, stored.shape, 1)
            stored = jnp.where(slots < len_ref[request], stored, -1e30)
            top = jnp.maximum(
                jnp.max(fresh, axis=-1, keepdims=True), jnp.max(stored, axis=-1, keepdims=True)
            )
            fresh, stored = jnp.exp(fresh - top), jnp.exp(stored - top)
            total = jnp.sum(fresh, axis=-1, keepdims=True) + jnp.sum(stored, axis=-1, keepdims=True)
            mixed = mix(fresh, v[own]) + mix(stored, cache_ref[request, 1, :, cut])
            outs.append((mixed / total).astype(jnp.bfloat16))
        heads.append(jnp.concatenate(outs, axis=0))
    out_ref[...] += jnp.dot(
        jnp.concatenate(heads, axis=1), w_out_ref[...], preferred_element_type=jnp.float32
    )


def attention(rows, gain, w_qkv, cache, cache_len, w_out):
    count, width = rows.shape
    units = w_qkv.shape[2]
    block = min(2 * HD, units)
    return pl.pallas_call(
        functools.partial(attention_kernel, 1.0 / math.sqrt(HD)),
        grid=(units // block,),
        in_specs=[
            pl.BlockSpec(memory_space=pltpu.SMEM),
            pl.BlockSpec((count, width), lambda i: (0, 0)),
            pl.BlockSpec((1, width), lambda i: (0, 0)),
            pl.BlockSpec((3, width, block), lambda i: (0, 0, i)),
            pl.BlockSpec((REQ_DEV, 2, CMAX, block), lambda i: (0, 0, 0, i)),
            pl.BlockSpec((block, width), lambda i: (i, 0)),
        ],
        out_specs=pl.BlockSpec((count, width), lambda i: (0, 0)),
        out_shape=jax.ShapeDtypeStruct((count, width), jnp.float32),
        scratch_shapes=[pltpu.VMEM((count, width), jnp.bfloat16)],
        compiler_params=pltpu.CompilerParams(vmem_limit_bytes=48 * 1024 * 1024),
        cost_estimate=pl.CostEstimate(
            flops=8 * count * width * units + 4 * PLEN * PLEN * units,
            bytes_accessed=8 * width * units + 6 * count * width,
            transcendentals=PLEN * PLEN * units // HD,
        ),
        name="attention",
    )(cache_len, rows, gain[None], jnp.transpose(w_qkv, (1, 0, 2)), cache, w_out)


def share_columns(share):
    high = share.astype(jnp.bfloat16)
    low = (share - high.astype(jnp.float32)).astype(jnp.bfloat16)
    spare = -2 * share.shape[1] % 128
    return jnp.concatenate([high, low, jnp.zeros((share.shape[0], spare), jnp.bfloat16)], axis=1)


def hidden_kernel(experts, width, me_ref, *refs):
    x_refs, weight_refs, out_refs = refs[:2], refs[2:-2], refs[-2:]
    units = weight_refs[0].shape[2]
    me = me_ref[0]
    for x_ref, out_ref in zip(x_refs, out_refs):
        extra = x_ref[:, width:].astype(jnp.float32)
        lanes = lax.broadcasted_iota(jnp.int32, extra.shape, 1)
        mine = (lanes == me) | (lanes == me + experts)
        share = jnp.sum(jnp.where(mine, extra, 0.0), axis=-1, keepdims=True)
        for part in range(len(weight_refs) // 2):
            gate_w, up_w = (r[...].reshape(width, units) for r in weight_refs[2 * part : 2 * part + 2])
            x = x_ref[:, :width]
            gate = jnp.dot(x, gate_w, preferred_element_type=jnp.float32)
            up = jnp.dot(x, up_w, preferred_element_type=jnp.float32)
            gate = 0.5 * gate
            out_ref[:, part * units : (part + 1) * units] = (
                (gate + gate * jnp.tanh(gate)) * (up * share)
            ).astype(jnp.bfloat16)


def expert_hidden(experts, me, blocks, weights):
    count = blocks[0].shape[0]
    sources, slice_width, units = weights[0].shape
    width, hidden = sources * slice_width, units * len(weights) // 2
    vmem = pl.BlockSpec(memory_space=pltpu.VMEM)
    out = jax.ShapeDtypeStruct((count, hidden), jnp.bfloat16)
    return pl.pallas_call(
        functools.partial(hidden_kernel, experts, width),
        in_specs=[pl.BlockSpec(memory_space=pltpu.SMEM)] + [vmem] * (2 + len(weights)),
        out_specs=[vmem] * 2,
        out_shape=[out, out],
        compiler_params=pltpu.CompilerParams(vmem_limit_bytes=16 * 1024 * 1024),
        cost_estimate=pl.CostEstimate(
            flops=8 * count * width * hidden,
            bytes_accessed=4 * count * (width + hidden) + 4 * width * hidden,
            transcendentals=2 * count * hidden,
        ),
        name="expert_hidden",
    )(me, *blocks, *weights)


def down_kernel(*refs):
    hidden_refs, weight_refs, out_refs = refs[:2], refs[2:-2], refs[-2:]
    sources, slice_width, units = weight_refs[0].shape
    group = max(1, min(sources, 1024 // slice_width))
    for hidden_ref, out_ref in zip(hidden_refs, out_refs):
        for first in range(0, sources, group):
            total = None
            for part, weight_ref in enumerate(weight_refs):
                term = lax.dot_general(
                    hidden_ref[:, part * units : (part + 1) * units],
                    weight_ref[first : first + group].reshape(group * slice_width, units),
                    (((1,), (1,)), ((), ())),
                    preferred_element_type=jnp.float32,
                )
                total = term if total is None else total + term
            cut = slice(first * slice_width, (first + group) * slice_width)
            out_ref[:, cut] = total.astype(jnp.bfloat16)


def expert_down(hiddens, weights):
    count, hidden = hiddens[0].shape
    width = weights[0].shape[0] * weights[0].shape[1]
    vmem = pl.BlockSpec(memory_space=pltpu.VMEM)
    out = jax.ShapeDtypeStruct((count, width), jnp.bfloat16)
    return pl.pallas_call(
        down_kernel,
        in_specs=[vmem] * (2 + len(weights)),
        out_specs=[vmem] * 2,
        out_shape=[out, out],
        compiler_params=pltpu.CompilerParams(vmem_limit_bytes=16 * 1024 * 1024),
        cost_estimate=pl.CostEstimate(
            flops=4 * count * width * hidden,
            bytes_accessed=4 * count * (width + hidden) + 2 * width * hidden,
            transcendentals=0,
        ),
        name="expert_down",
    )(*hiddens, *weights)


def sum_kernel(cut, refs):
    total = refs[0][:, cut].astype(jnp.float32) + refs[1][:, cut].astype(jnp.float32)
    for ref in refs[2:-1]:
        total = total + ref[...].astype(jnp.float32)
    refs[-1][...] = total.astype(jnp.bfloat16)


def add_terms(cut, keep, got, running):
    terms = [keep, got] + ([] if running is None else [running])
    columns = cut.stop - cut.start
    vmem = pl.BlockSpec(memory_space=pltpu.VMEM)
    return pl.pallas_call(
        lambda *refs: sum_kernel(cut, refs),
        in_specs=[vmem] * len(terms),
        out_specs=vmem,
        out_shape=jax.ShapeDtypeStruct((keep.shape[0], columns), jnp.bfloat16),
        compiler_params=pltpu.CompilerParams(vmem_limit_bytes=16 * 1024 * 1024),
        cost_estimate=pl.CostEstimate(
            flops=2 * keep.shape[0] * columns,
            bytes_accessed=8 * keep.shape[0] * columns,
            transcendentals=0,
        ),
        name="add_terms",
    )(*terms)


def chip_ring(chips):
    rows = 4
    columns = chips // rows
    if chips % rows or columns < 2:
        return list(range(chips))
    order = [z * columns for z in range(rows)]
    for turn, z in enumerate(reversed(range(rows))):
        line = [z * columns + x for x in range(1, columns)]
        order += line if turn % 2 == 0 else line[::-1]
    return order


def on_device(
    x_tokens,
    attn_gain,
    w_qkv,
    w_out,
    cache,
    cache_len,
    moe_gain,
    w_trainer,
    expert_ids,
    route_probs,
):
    kv, ex = lax.axis_size("kv"), lax.axis_size("ex")
    me, me_kv = lax.axis_index("ex"), lax.axis_index("kv")
    experts = w_trainer.shape[0]

    def over_experts(part):
        return lax.all_to_all(part, "ex", split_axis=0, concat_axis=0, tiled=True)

    def over_kv(part):
        middle = part.shape[0] // 2
        return [
            [
                lax.ppermute(half, "kv", [(i, (i + turn) % kv) for i in range(kv)])
                for turn in range(1, kv)
            ]
            for half in (part[:middle], part[middle:])
        ]

    def joined(halves):
        return [jnp.concatenate(pair, axis=0) for pair in zip(*halves)]

    probs = route_probs[0]
    share = probs / jnp.sum(probs, axis=-1, keepdims=True)
    named = expert_ids[0][:, :, None] == jnp.arange(experts, dtype=jnp.int32)[None, None, :]
    factor = jnp.sum(jnp.where(named, share[:, :, None], 0.0), axis=1)
    factor = share_columns(factor)

    rows = x_tokens[0]
    row_count = rows.shape[0]
    rows_dev = row_count // kv
    gate = w_trainer[:, 0].astype(jnp.bfloat16)
    gate, rest = lax.optimization_barrier((gate, w_trainer))
    up, down = (rest[:, kind].astype(jnp.bfloat16) for kind in (1, 2))
    gate = over_experts(gate)
    mixed = attention(rows, attn_gain, w_qkv, cache, cache_len, w_out)
    mixed, gate, up, down = lax.optimization_barrier((mixed, gate, up, down))
    gates = over_kv(gate)
    up = over_experts(up)
    mixed = mixed.reshape(kv, rows_dev, mixed.shape[1])

    def rows_of(part):
        return lax.dynamic_index_in_dim(mixed, part, 0, keepdims=False)

    own_rows = lax.dynamic_slice_in_dim(rows, me_kv * rows_dev, rows_dev, 0)
    resid = own_rows.astype(jnp.float32) + rows_of(me_kv)
    for turn in range(1, kv):
        sent = rows_of(lax.rem(me_kv + turn, kv)).astype(jnp.bfloat16)
        sent = lax.ppermute(sent, "kv", [(i, (i + turn) % kv) for i in range(kv)])
        resid = resid + sent.astype(jnp.float32)
    moe_in = rms_scale(resid, moe_gain).astype(jnp.bfloat16)
    moe_in = jnp.concatenate([moe_in, factor], axis=1)
    moe_in, gates[0], up, down = lax.optimization_barrier((moe_in, gates[0], up, down))
    ups = over_kv(up)
    down = over_experts(down)

    cores = 2
    order = chip_ring(ex // cores)
    chips = len(order)
    half = rows_dev // 2
    core = lax.rem(me, cores)
    ring, swap = [], [(i, i ^ 1) for i in range(ex)]
    for spot, chip in enumerate(order):
        for c in range(cores):
            here = chip * cores + c
            ring.append((here, order[(spot + 1 - 2 * c) % chips] * cores + c))

    def half_of(array, which):
        return lax.dynamic_slice_in_dim(array, which * half, half, 0)

    got = lax.ppermute(half_of(moe_in, 1 - core), "ex", swap)
    held = jnp.concatenate([half_of(moe_in, core), got], axis=0)
    first_weights = [gate, up]
    due = {4: [0], 5: [1, 2], 6: [3], 7: [4]}
    blocks, hiddens = [held], {}

    def hidden_of(step):
        other = lax.ppermute(blocks[step], "ex", swap)
        return expert_hidden(experts, me[None], [blocks[step], other], first_weights)

    for step in range(1, chips):
        held = lax.ppermute(held, "ex", ring)
        if step == 1:
            held, gates[1] = lax.optimization_barrier((held, gates[1]))
        if step == 2:
            held, ups, down = lax.optimization_barrier((held, ups, down))
            downs = over_kv(down)
            for pair in zip(joined(gates), joined(ups)):
                first_weights += pair
        blocks.append(held)
        for early in due.get(step, []):
            hiddens[early] = hidden_of(early)
            held, hiddens[early] = lax.optimization_barrier((held, hiddens[early]))
        blocks[step] = held
    for step in range(chips):
        if step not in hiddens:
            hiddens[step] = hidden_of(step)
    hiddens = [hiddens[step] for step in range(chips)]
    downs = joined(downs)
    keeps, gots = [], []
    for pair in hiddens:
        keep, give = expert_down(pair, [down] + downs)
        keeps.append(keep)
        gots.append(lax.ppermute(give, "ex", swap))

    width = w_out.shape[1]
    sums = []
    for cut in (slice(0, width // 2), slice(width // 2, width)):
        running = None
        for step in list(range(1, chips)) + [0]:
            running = add_terms(cut, keeps[step], gots[step], running)
            if step:
                running = lax.ppermute(running, "ex", ring)
        sums.append(running)
    running = jnp.concatenate(sums, axis=1)
    got = lax.ppermute(running[half:], "ex", swap)
    moe_out = jnp.where(
        core == 0,
        jnp.concatenate([running[:half], got], axis=0),
        jnp.concatenate([got, running[:half]], axis=0),
    )
    return (resid + moe_out.astype(jnp.float32)).astype(jnp.bfloat16)[None]


def solution(mesh):
    return jax.shard_map(
        on_device,
        mesh=mesh,
        in_specs=(
            P("ex", None, None),
            P(),
            P(None, None, "kv"),
            P("kv", None),
            P("ex", None, None, "kv"),
            P("ex"),
            P(),
            P(None, None, "ex", "kv"),
            P("ex", "kv", None),
            P("ex", "kv", None),
        ),
        out_specs=P("ex", "kv", None),
        check_vma=False,
    )
```

```python
import functools
import math

import jax
import jax.numpy as jnp
from jax import lax
from jax.experimental import pallas as pl
from jax.experimental.pallas import tpu as pltpu
from jax.sharding import PartitionSpec as P

HD = 128
TOPK = 8
PLEN = 512
REQ_DEV = 2
QB = 32
CMAX = 512


def rms_scale(rows, gain):
    values = rows.astype(jnp.float32)
    scale = lax.rsqrt(jnp.mean(values * values, axis=-1, keepdims=True) + 1e-06)
    return values * scale * gain


def attention_kernel(scale, len_ref, x_ref, gain_ref, w_ref, cache_ref, w_out_ref, out_ref, normed):
    @pl.when(pl.program_id(0) == 0)
    def _():
        normed[...] = rms_scale(x_ref[...], gain_ref[...]).astype(jnp.bfloat16)
        out_ref[...] = jnp.zeros_like(out_ref)

    rows = normed[...]
    query, keys, values = (
        jnp.dot(rows, w_ref[j], preferred_element_type=jnp.float32).astype(jnp.bfloat16)
        for j in range(3)
    )

    def scores_of(q, k):
        return scale * lax.dot_general(
            q, k, (((1,), (1,)), ((), ())), preferred_element_type=jnp.float32
        )

    def mix(weights, v):
        return jnp.dot(weights.astype(jnp.bfloat16), v, preferred_element_type=jnp.float32)

    heads = []
    for head in range(query.shape[1] // HD):
        cut = slice(head * HD, (head + 1) * HD)
        q, k, v = query[:, cut], keys[:, cut], values[:, cut]
        scores = scores_of(q[:PLEN], k[:PLEN])
        weights = jnp.exp(scores - jnp.max(scores, axis=-1, keepdims=True))
        total = jnp.sum(weights, axis=-1, keepdims=True)
        outs = [(mix(weights, v[:PLEN]) / total).astype(jnp.bfloat16)]
        for request in range(REQ_DEV):
            own = slice(PLEN + request * QB, PLEN + (request + 1) * QB)
            fresh = scores_of(q[own], k[own])
            stored = scores_of(q[own], cache_ref[request, 0, :, cut])
            slots = lax.broadcasted_iota(jnp.int32, stored.shape, 1)
            stored = jnp.where(slots < len_ref[request], stored, -1e30)
            top = jnp.maximum(
                jnp.max(fresh, axis=-1, keepdims=True), jnp.max(stored, axis=-1, keepdims=True)
            )
            fresh, stored = jnp.exp(fresh - top), jnp.exp(stored - top)
            total = jnp.sum(fresh, axis=-1, keepdims=True) + jnp.sum(stored, axis=-1, keepdims=True)
            mixed = mix(fresh, v[own]) + mix(stored, cache_ref[request, 1, :, cut])
            outs.append((mixed / total).astype(jnp.bfloat16))
        heads.append(jnp.concatenate(outs, axis=0))
    out_ref[...] += jnp.dot(
        jnp.concatenate(heads, axis=1), w_out_ref[...], preferred_element_type=jnp.float32
    )


def attention(rows, gain, w_qkv, cache, cache_len, w_out):
    count, width = rows.shape
    units = w_qkv.shape[2]
    block = min(2 * HD, units)
    return pl.pallas_call(
        functools.partial(attention_kernel, 1.0 / math.sqrt(HD)),
        grid=(units // block,),
        in_specs=[
            pl.BlockSpec(memory_space=pltpu.SMEM),
            pl.BlockSpec((count, width), lambda i: (0, 0)),
            pl.BlockSpec((1, width), lambda i: (0, 0)),
            pl.BlockSpec((3, width, block), lambda i: (0, 0, i)),
            pl.BlockSpec((REQ_DEV, 2, CMAX, block), lambda i: (0, 0, 0, i)),
            pl.BlockSpec((block, width), lambda i: (i, 0)),
        ],
        out_specs=pl.BlockSpec((count, width), lambda i: (0, 0)),
        out_shape=jax.ShapeDtypeStruct((count, width), jnp.float32),
        scratch_shapes=[pltpu.VMEM((count, width), jnp.bfloat16)],
        compiler_params=pltpu.CompilerParams(vmem_limit_bytes=48 * 1024 * 1024),
        cost_estimate=pl.CostEstimate(
            flops=8 * count * width * units + 4 * PLEN * PLEN * units,
            bytes_accessed=8 * width * units + 6 * count * width,
            transcendentals=PLEN * PLEN * units // HD,
        ),
        name="attention",
    )(cache_len, rows, gain[None], jnp.transpose(w_qkv, (1, 0, 2)), cache, w_out)


def share_columns(share):
    high = share.astype(jnp.bfloat16)
    low = (share - high.astype(jnp.float32)).astype(jnp.bfloat16)
    spare = -2 * share.shape[1] % 128
    return jnp.concatenate([high, low, jnp.zeros((share.shape[0], spare), jnp.bfloat16)], axis=1)


def hidden_kernel(experts, width, me_ref, *refs):
    x_refs, weight_refs, out_refs = refs[:2], refs[2:-2], refs[-2:]
    units = weight_refs[0].shape[2]
    me = me_ref[0]
    for x_ref, out_ref in zip(x_refs, out_refs):
        extra = x_ref[:, width:].astype(jnp.float32)
        lanes = lax.broadcasted_iota(jnp.int32, extra.shape, 1)
        mine = (lanes == me) | (lanes == me + experts)
        share = jnp.sum(jnp.where(mine, extra, 0.0), axis=-1, keepdims=True)
        for part in range(len(weight_refs) // 2):
            gate_w, up_w = (r[...].reshape(width, units) for r in weight_refs[2 * part : 2 * part + 2])
            x = x_ref[:, :width]
            gate = jnp.dot(x, gate_w, preferred_element_type=jnp.float32)
            up = jnp.dot(x, up_w, preferred_element_type=jnp.float32)
            gate = 0.5 * gate
            out_ref[:, part * units : (part + 1) * units] = (
                (gate + gate * jnp.tanh(gate)) * (up * share)
            ).astype(jnp.bfloat16)


def expert_hidden(experts, me, blocks, weights):
    count = blocks[0].shape[0]
    sources, slice_width, units = weights[0].shape
    width, hidden = sources * slice_width, units * len(weights) // 2
    vmem = pl.BlockSpec(memory_space=pltpu.VMEM)
    out = jax.ShapeDtypeStruct((count, hidden), jnp.bfloat16)
    return pl.pallas_call(
        functools.partial(hidden_kernel, experts, width),
        in_specs=[pl.BlockSpec(memory_space=pltpu.SMEM)] + [vmem] * (2 + len(weights)),
        out_specs=[vmem] * 2,
        out_shape=[out, out],
        compiler_params=pltpu.CompilerParams(vmem_limit_bytes=16 * 1024 * 1024),
        cost_estimate=pl.CostEstimate(
            flops=8 * count * width * hidden,
            bytes_accessed=4 * count * (width + hidden) + 4 * width * hidden,
            transcendentals=2 * count * hidden,
        ),
        name="expert_hidden",
    )(me, *blocks, *weights)


def down_kernel(*refs):
    hidden_refs, weight_refs, out_refs = refs[:2], refs[2:-2], refs[-2:]
    sources, slice_width, units = weight_refs[0].shape
    group = max(1, min(sources, 1024 // slice_width))
    for hidden_ref, out_ref in zip(hidden_refs, out_refs):
        for first in range(0, sources, group):
            total = None
            for part, weight_ref in enumerate(weight_refs):
                term = lax.dot_general(
                    hidden_ref[:, part * units : (part + 1) * units],
                    weight_ref[first : first + group].reshape(group * slice_width, units),
                    (((1,), (1,)), ((), ())),
                    preferred_element_type=jnp.float32,
                )
                total = term if total is None else total + term
            cut = slice(first * slice_width, (first + group) * slice_width)
            out_ref[:, cut] = total.astype(jnp.bfloat16)


def expert_down(hiddens, weights):
    count, hidden = hiddens[0].shape
    width = weights[0].shape[0] * weights[0].shape[1]
    vmem = pl.BlockSpec(memory_space=pltpu.VMEM)
    out = jax.ShapeDtypeStruct((count, width), jnp.bfloat16)
    return pl.pallas_call(
        down_kernel,
        in_specs=[vmem] * (2 + len(weights)),
        out_specs=[vmem] * 2,
        out_shape=[out, out],
        compiler_params=pltpu.CompilerParams(vmem_limit_bytes=16 * 1024 * 1024),
        cost_estimate=pl.CostEstimate(
            flops=4 * count * width * hidden,
            bytes_accessed=4 * count * (width + hidden) + 2 * width * hidden,
            transcendentals=0,
        ),
        name="expert_down",
    )(*hiddens, *weights)


def sum_kernel(cut, refs):
    total = refs[0][:, cut].astype(jnp.float32) + refs[1][:, cut].astype(jnp.float32)
    for ref in refs[2:-1]:
        total = total + ref[...].astype(jnp.float32)
    refs[-1][...] = total.astype(jnp.bfloat16)


def add_terms(cut, keep, got, running):
    terms = [keep, got] + ([] if running is None else [running])
    columns = cut.stop - cut.start
    vmem = pl.BlockSpec(memory_space=pltpu.VMEM)
    return pl.pallas_call(
        lambda *refs: sum_kernel(cut, refs),
        in_specs=[vmem] * len(terms),
        out_specs=vmem,
        out_shape=jax.ShapeDtypeStruct((keep.shape[0], columns), jnp.bfloat16),
        compiler_params=pltpu.CompilerParams(vmem_limit_bytes=16 * 1024 * 1024),
        cost_estimate=pl.CostEstimate(
            flops=2 * keep.shape[0] * columns,
            bytes_accessed=8 * keep.shape[0] * columns,
            transcendentals=0,
        ),
        name="add_terms",
    )(*terms)


def chip_ring(chips):
    rows = 4
    columns = chips // rows
    if chips % rows or columns < 2:
        return list(range(chips))
    order = [z * columns for z in range(rows)]
    for turn, z in enumerate(reversed(range(rows))):
        line = [z * columns + x for x in range(1, columns)]
        order += line if turn % 2 == 0 else line[::-1]
    return order


def on_device(
    x_tokens,
    attn_gain,
    w_qkv,
    w_out,
    cache,
    cache_len,
    moe_gain,
    w_trainer,
    expert_ids,
    route_probs,
):
    kv, ex = lax.axis_size("kv"), lax.axis_size("ex")
    me, me_kv = lax.axis_index("ex"), lax.axis_index("kv")
    experts = w_trainer.shape[0]

    def over_experts(part):
        return lax.all_to_all(part, "ex", split_axis=0, concat_axis=0, tiled=True)

    def over_kv(part):
        return [
            lax.ppermute(part, "kv", [(i, (i + turn) % kv) for i in range(kv)])
            for turn in range(1, kv)
        ]

    probs = route_probs[0]
    share = probs / jnp.sum(probs, axis=-1, keepdims=True)
    named = expert_ids[0][:, :, None] == jnp.arange(experts, dtype=jnp.int32)[None, None, :]
    factor = jnp.sum(jnp.where(named, share[:, :, None], 0.0), axis=1)
    factor = share_columns(factor)

    rows = x_tokens[0]
    row_count = rows.shape[0]
    rows_dev = row_count // kv
    gate = w_trainer[:, 0].astype(jnp.bfloat16)
    gate, rest = lax.optimization_barrier((gate, w_trainer))
    up, down = (rest[:, kind].astype(jnp.bfloat16) for kind in (1, 2))
    gate = over_experts(gate)
    mixed = attention(rows, attn_gain, w_qkv, cache, cache_len, w_out)
    mixed, gate, up, down = lax.optimization_barrier((mixed, gate, up, down))
    gates = over_kv(gate)
    up = over_experts(up)
    mixed = mixed.reshape(kv, rows_dev, mixed.shape[1])

    def rows_of(part):
        return lax.dynamic_index_in_dim(mixed, part, 0, keepdims=False)

    own_rows = lax.dynamic_slice_in_dim(rows, me_kv * rows_dev, rows_dev, 0)
    resid = own_rows.astype(jnp.float32) + rows_of(me_kv)
    for turn in range(1, kv):
        sent = rows_of(lax.rem(me_kv + turn, kv)).astype(jnp.bfloat16)
        sent = lax.ppermute(sent, "kv", [(i, (i + turn) % kv) for i in range(kv)])
        resid = resid + sent.astype(jnp.float32)
    moe_in = rms_scale(resid, moe_gain).astype(jnp.bfloat16)
    moe_in = jnp.concatenate([moe_in, factor], axis=1)
    moe_in, up, down = lax.optimization_barrier((moe_in, up, down))
    ups = over_kv(up)
    down = over_experts(down)

    cores = 2
    order = chip_ring(ex // cores)
    chips = len(order)
    half = rows_dev // 2
    core = lax.rem(me, cores)
    ring, swap = [], [(i, i ^ 1) for i in range(ex)]
    for spot, chip in enumerate(order):
        for c in range(cores):
            here = chip * cores + c
            ring.append((here, order[(spot + 1 - 2 * c) % chips] * cores + c))

    def half_of(array, which):
        return lax.dynamic_slice_in_dim(array, which * half, half, 0)

    got = lax.ppermute(half_of(moe_in, 1 - core), "ex", swap)
    held = jnp.concatenate([half_of(moe_in, core), got], axis=0)
    first_weights = [gate, up]
    due = {3: [0], 4: [1], 5: [2], 6: [3], 7: [4]}
    blocks, hiddens = [held], {}

    def hidden_of(step):
        other = lax.ppermute(blocks[step], "ex", swap)
        return expert_hidden(experts, me[None], [blocks[step], other], first_weights)

    for step in range(1, chips):
        held = lax.ppermute(held, "ex", ring)
        if step == 1:
            held, gates = lax.optimization_barrier((held, gates))
        if step == 2:
            held, ups, down = lax.optimization_barrier((held, ups, down))
            downs = over_kv(down)
            for pair in zip(gates, ups):
                first_weights += pair
        if step == min(4, chips - 1):
            held, downs = lax.optimization_barrier((held, downs))
        blocks.append(held)
        for early in due.get(step, []):
            hiddens[early] = hidden_of(early)
            held, hiddens[early] = lax.optimization_barrier((held, hiddens[early]))
        blocks[step] = held
    for step in range(chips):
        if step not in hiddens:
            hiddens[step] = hidden_of(step)
    hiddens = [hiddens[step] for step in range(chips)]
    keeps, gots = [], []
    for pair in hiddens:
        keep, give = expert_down(pair, [down] + downs)
        keeps.append(keep)
        gots.append(lax.ppermute(give, "ex", swap))

    width = w_out.shape[1]
    sums = []
    for cut in (slice(0, width // 2), slice(width // 2, width)):
        running = None
        for step in list(range(1, chips)) + [0]:
            running = add_terms(cut, keeps[step], gots[step], running)
            if step:
                running = lax.ppermute(running, "ex", ring)
        sums.append(running)
    running = jnp.concatenate(sums, axis=1)
    got = lax.ppermute(running[half:], "ex", swap)
    moe_out = jnp.where(
        core == 0,
        jnp.concatenate([running[:half], got], axis=0),
        jnp.concatenate([got, running[:half]], axis=0),
    )
    return (resid + moe_out.astype(jnp.float32)).astype(jnp.bfloat16)[None]


def solution(mesh):
    return jax.shard_map(
        on_device,
        mesh=mesh,
        in_specs=(
            P("ex", None, None),
            P(),
            P(None, None, "kv"),
            P("kv", None),
            P("ex", None, None, "kv"),
            P("ex"),
            P(),
            P(None, None, "ex", "kv"),
            P("ex", "kv", None),
            P("ex", "kv", None),
        ),
        out_specs=P("ex", "kv", None),
        check_vma=False,
    )
```

```python
import functools
import math

import jax
import jax.numpy as jnp
from jax import lax
from jax.experimental import pallas as pl
from jax.experimental.pallas import tpu as pltpu
from jax.sharding import PartitionSpec as P

HD = 128
TOPK = 8
PLEN = 512
REQ_DEV = 2
QB = 32
CMAX = 512


def rms_scale(rows, gain):
    values = rows.astype(jnp.float32)
    scale = lax.rsqrt(jnp.mean(values * values, axis=-1, keepdims=True) + 1e-06)
    return values * scale * gain


def attention_kernel(scale, len_ref, x_ref, gain_ref, w_ref, cache_ref, w_out_ref, out_ref, normed):
    @pl.when(pl.program_id(0) == 0)
    def _():
        normed[...] = rms_scale(x_ref[...], gain_ref[...]).astype(jnp.bfloat16)
        out_ref[...] = jnp.zeros_like(out_ref)

    rows = normed[...]
    query, keys, values = (
        jnp.dot(rows, w_ref[j], preferred_element_type=jnp.float32).astype(jnp.bfloat16)
        for j in range(3)
    )

    def scores_of(q, k):
        return scale * lax.dot_general(
            q, k, (((1,), (1,)), ((), ())), preferred_element_type=jnp.float32
        )

    def mix(weights, v):
        return jnp.dot(weights.astype(jnp.bfloat16), v, preferred_element_type=jnp.float32)

    heads = []
    for head in range(query.shape[1] // HD):
        cut = slice(head * HD, (head + 1) * HD)
        q, k, v = query[:, cut], keys[:, cut], values[:, cut]
        scores = scores_of(q[:PLEN], k[:PLEN])
        weights = jnp.exp(scores - jnp.max(scores, axis=-1, keepdims=True))
        total = jnp.sum(weights, axis=-1, keepdims=True)
        outs = [(mix(weights, v[:PLEN]) / total).astype(jnp.bfloat16)]
        for request in range(REQ_DEV):
            own = slice(PLEN + request * QB, PLEN + (request + 1) * QB)
            fresh = scores_of(q[own], k[own])
            stored = scores_of(q[own], cache_ref[request, 0, :, cut])
            slots = lax.broadcasted_iota(jnp.int32, stored.shape, 1)
            stored = jnp.where(slots < len_ref[request], stored, -1e30)
            top = jnp.maximum(
                jnp.max(fresh, axis=-1, keepdims=True), jnp.max(stored, axis=-1, keepdims=True)
            )
            fresh, stored = jnp.exp(fresh - top), jnp.exp(stored - top)
            total = jnp.sum(fresh, axis=-1, keepdims=True) + jnp.sum(stored, axis=-1, keepdims=True)
            mixed = mix(fresh, v[own]) + mix(stored, cache_ref[request, 1, :, cut])
            outs.append((mixed / total).astype(jnp.bfloat16))
        heads.append(jnp.concatenate(outs, axis=0))
    out_ref[...] += jnp.dot(
        jnp.concatenate(heads, axis=1), w_out_ref[...], preferred_element_type=jnp.float32
    )


def attention(rows, gain, w_qkv, cache, cache_len, w_out):
    count, width = rows.shape
    units = w_qkv.shape[2]
    block = min(2 * HD, units)
    return pl.pallas_call(
        functools.partial(attention_kernel, 1.0 / math.sqrt(HD)),
        grid=(units // block,),
        in_specs=[
            pl.BlockSpec(memory_space=pltpu.SMEM),
            pl.BlockSpec((count, width), lambda i: (0, 0)),
            pl.BlockSpec((1, width), lambda i: (0, 0)),
            pl.BlockSpec((3, width, block), lambda i: (0, 0, i)),
            pl.BlockSpec((REQ_DEV, 2, CMAX, block), lambda i: (0, 0, 0, i)),
            pl.BlockSpec((block, width), lambda i: (i, 0)),
        ],
        out_specs=pl.BlockSpec((count, width), lambda i: (0, 0)),
        out_shape=jax.ShapeDtypeStruct((count, width), jnp.float32),
        scratch_shapes=[pltpu.VMEM((count, width), jnp.bfloat16)],
        compiler_params=pltpu.CompilerParams(vmem_limit_bytes=38 * 1024 * 1024),
        cost_estimate=pl.CostEstimate(
            flops=8 * count * width * units + 4 * PLEN * PLEN * units,
            bytes_accessed=8 * width * units + 6 * count * width,
            transcendentals=PLEN * PLEN * units // HD,
        ),
        name="attention",
    )(cache_len, rows, gain[None], jnp.transpose(w_qkv, (1, 0, 2)), cache, w_out)


def share_columns(share):
    high = share.astype(jnp.bfloat16)
    low = (share - high.astype(jnp.float32)).astype(jnp.bfloat16)
    spare = -2 * share.shape[1] % 128
    return jnp.concatenate([high, low, jnp.zeros((share.shape[0], spare), jnp.bfloat16)], axis=1)


def hidden_kernel(experts, width, me_ref, *refs):
    x_refs, weight_refs, out_refs = refs[:2], refs[2:-2], refs[-2:]
    units = weight_refs[0].shape[2]
    me = me_ref[0]
    for x_ref, out_ref in zip(x_refs, out_refs):
        extra = x_ref[:, width:].astype(jnp.float32)
        lanes = lax.broadcasted_iota(jnp.int32, extra.shape, 1)
        mine = (lanes == me) | (lanes == me + experts)
        share = jnp.sum(jnp.where(mine, extra, 0.0), axis=-1, keepdims=True)
        for part in range(len(weight_refs) // 2):
            gate_w, up_w = (r[...].reshape(width, units) for r in weight_refs[2 * part : 2 * part + 2])
            x = x_ref[:, :width]
            gate = jnp.dot(x, gate_w, preferred_element_type=jnp.float32)
            up = jnp.dot(x, up_w, preferred_element_type=jnp.float32)
            gate = 0.5 * gate
            out_ref[:, part * units : (part + 1) * units] = (
                (gate + gate * jnp.tanh(gate)) * (up * share)
            ).astype(jnp.bfloat16)


def expert_hidden(experts, me, blocks, weights):
    count = blocks[0].shape[0]
    sources, slice_width, units = weights[0].shape
    width, hidden = sources * slice_width, units * len(weights) // 2
    vmem = pl.BlockSpec(memory_space=pltpu.VMEM)
    out = jax.ShapeDtypeStruct((count, hidden), jnp.bfloat16)
    return pl.pallas_call(
        functools.partial(hidden_kernel, experts, width),
        in_specs=[pl.BlockSpec(memory_space=pltpu.SMEM)] + [vmem] * (2 + len(weights)),
        out_specs=[vmem] * 2,
        out_shape=[out, out],
        compiler_params=pltpu.CompilerParams(vmem_limit_bytes=8 * 1024 * 1024),
        cost_estimate=pl.CostEstimate(
            flops=8 * count * width * hidden,
            bytes_accessed=4 * count * (width + hidden) + 4 * width * hidden,
            transcendentals=2 * count * hidden,
        ),
        name="expert_hidden",
    )(me, *blocks, *weights)


def down_kernel(*refs):
    hidden_refs, weight_refs, out_refs = refs[:2], refs[2:-2], refs[-2:]
    sources, slice_width, units = weight_refs[0].shape
    group = max(1, min(sources, 1024 // slice_width))
    for hidden_ref, out_ref in zip(hidden_refs, out_refs):
        for first in range(0, sources, group):
            total = None
            for part, weight_ref in enumerate(weight_refs):
                term = lax.dot_general(
                    hidden_ref[:, part * units : (part + 1) * units],
                    weight_ref[first : first + group].reshape(group * slice_width, units),
                    (((1,), (1,)), ((), ())),
                    preferred_element_type=jnp.float32,
                )
                total = term if total is None else total + term
            cut = slice(first * slice_width, (first + group) * slice_width)
            out_ref[:, cut] = total.astype(jnp.bfloat16)


def expert_down(hiddens, weights):
    count, hidden = hiddens[0].shape
    width = weights[0].shape[0] * weights[0].shape[1]
    vmem = pl.BlockSpec(memory_space=pltpu.VMEM)
    out = jax.ShapeDtypeStruct((count, width), jnp.bfloat16)
    return pl.pallas_call(
        down_kernel,
        in_specs=[vmem] * (2 + len(weights)),
        out_specs=[vmem] * 2,
        out_shape=[out, out],
        compiler_params=pltpu.CompilerParams(vmem_limit_bytes=8 * 1024 * 1024),
        cost_estimate=pl.CostEstimate(
            flops=4 * count * width * hidden,
            bytes_accessed=4 * count * (width + hidden) + 2 * width * hidden,
            transcendentals=0,
        ),
        name="expert_down",
    )(*hiddens, *weights)


def sum_kernel(cut, refs):
    total = refs[0][:, cut].astype(jnp.float32) + refs[1][:, cut].astype(jnp.float32)
    for ref in refs[2:-1]:
        total = total + ref[...].astype(jnp.float32)
    refs[-1][...] = total.astype(jnp.bfloat16)


def add_terms(cut, keep, got, running):
    terms = [keep, got] + ([] if running is None else [running])
    columns = cut.stop - cut.start
    vmem = pl.BlockSpec(memory_space=pltpu.VMEM)
    return pl.pallas_call(
        lambda *refs: sum_kernel(cut, refs),
        in_specs=[vmem] * len(terms),
        out_specs=vmem,
        out_shape=jax.ShapeDtypeStruct((keep.shape[0], columns), jnp.bfloat16),
        compiler_params=pltpu.CompilerParams(vmem_limit_bytes=8 * 1024 * 1024),
        cost_estimate=pl.CostEstimate(
            flops=2 * keep.shape[0] * columns,
            bytes_accessed=8 * keep.shape[0] * columns,
            transcendentals=0,
        ),
        name="add_terms",
    )(*terms)


def chip_ring(chips):
    rows = 4
    columns = chips // rows
    if chips % rows or columns < 2:
        return list(range(chips))
    order = [z * columns for z in range(rows)]
    for turn, z in enumerate(reversed(range(rows))):
        line = [z * columns + x for x in range(1, columns)]
        order += line if turn % 2 == 0 else line[::-1]
    return order


def on_device(
    x_tokens,
    attn_gain,
    w_qkv,
    w_out,
    cache,
    cache_len,
    moe_gain,
    w_trainer,
    expert_ids,
    route_probs,
):
    kv, ex = lax.axis_size("kv"), lax.axis_size("ex")
    me, me_kv = lax.axis_index("ex"), lax.axis_index("kv")
    experts = w_trainer.shape[0]

    def over_experts(part):
        return lax.all_to_all(part, "ex", split_axis=0, concat_axis=0, tiled=True)

    def over_kv(part):
        return [
            lax.ppermute(part, "kv", [(i, (i + turn) % kv) for i in range(kv)])
            for turn in range(1, kv)
        ]

    probs = route_probs[0]
    share = probs / jnp.sum(probs, axis=-1, keepdims=True)
    named = expert_ids[0][:, :, None] == jnp.arange(experts, dtype=jnp.int32)[None, None, :]
    factor = jnp.sum(jnp.where(named, share[:, :, None], 0.0), axis=1)
    factor = share_columns(factor)

    rows = x_tokens[0]
    row_count = rows.shape[0]
    rows_dev = row_count // kv
    gate = w_trainer[:, 0].astype(jnp.bfloat16)
    gate, rest = lax.optimization_barrier((gate, w_trainer))
    up, down = (rest[:, kind].astype(jnp.bfloat16) for kind in (1, 2))
    gate = over_experts(gate)
    mixed = attention(rows, attn_gain, w_qkv, cache, cache_len, w_out)
    mixed, gate, up, down = lax.optimization_barrier((mixed, gate, up, down))
    gates = over_kv(gate)
    up = over_experts(up)
    mixed = mixed.reshape(kv, rows_dev, mixed.shape[1])

    def rows_of(part):
        return lax.dynamic_index_in_dim(mixed, part, 0, keepdims=False)

    own_rows = lax.dynamic_slice_in_dim(rows, me_kv * rows_dev, rows_dev, 0)
    resid = own_rows.astype(jnp.float32) + rows_of(me_kv)
    for turn in range(1, kv):
        sent = rows_of(lax.rem(me_kv + turn, kv)).astype(jnp.bfloat16)
        sent = lax.ppermute(sent, "kv", [(i, (i + turn) % kv) for i in range(kv)])
        resid = resid + sent.astype(jnp.float32)
    resid, up, down = lax.optimization_barrier((resid, up, down))
    ups = over_kv(up)
    down = over_experts(down)
    moe_in = rms_scale(resid, moe_gain).astype(jnp.bfloat16)
    moe_in = jnp.concatenate([moe_in, factor], axis=1)

    cores = 2
    order = chip_ring(ex // cores)
    chips = len(order)
    half = rows_dev // 2
    core = lax.rem(me, cores)
    ring, swap = [], [(i, i ^ 1) for i in range(ex)]
    for spot, chip in enumerate(order):
        for c in range(cores):
            here = chip * cores + c
            ring.append((here, order[(spot + 1 - 2 * c) % chips] * cores + c))

    def half_of(array, which):
        return lax.dynamic_slice_in_dim(array, which * half, half, 0)

    got = lax.ppermute(half_of(moe_in, 1 - core), "ex", swap)
    held = jnp.concatenate([half_of(moe_in, core), got], axis=0)
    first_weights = [gate, up]
    due = {3: [0, 1], 4: [2, 3], 5: [4], 6: [5], 7: [6]}
    held, gates = lax.optimization_barrier((held, gates))
    blocks, hiddens = [held], {}

    def hidden_of(step):
        other = lax.ppermute(blocks[step], "ex", swap)
        return expert_hidden(experts, me[None], [blocks[step], other], first_weights)

    for step in range(1, chips):
        held = lax.ppermute(held, "ex", ring)
        if step == 2:
            held, ups, down = lax.optimization_barrier((held, ups, down))
            downs = over_kv(down)
            for pair in zip(gates, ups):
                first_weights += pair
        blocks.append(held)
        for early in due.get(step, []):
            hiddens[early] = hidden_of(early)
            held, hiddens[early] = lax.optimization_barrier((held, hiddens[early]))
        if step == min(4, chips - 1):
            held, downs = lax.optimization_barrier((held, downs))
        blocks[step] = held
    for step in range(chips):
        if step not in hiddens:
            hiddens[step] = hidden_of(step)
    hiddens = [hiddens[step] for step in range(chips)]
    keeps, gots = [], []
    for pair in hiddens:
        keep, give = expert_down(pair, [down] + downs)
        keeps.append(keep)
        gots.append(lax.ppermute(give, "ex", swap))

    width = w_out.shape[1]
    sums = []
    for cut in (slice(0, width // 2), slice(width // 2, width)):
        running = None
        for step in list(range(1, chips)) + [0]:
            running = add_terms(cut, keeps[step], gots[step], running)
            if step:
                running = lax.ppermute(running, "ex", ring)
        sums.append(running)
    running = jnp.concatenate(sums, axis=1)
    got = lax.ppermute(running[half:], "ex", swap)
    moe_out = jnp.where(
        core == 0,
        jnp.concatenate([running[:half], got], axis=0),
        jnp.concatenate([got, running[:half]], axis=0),
    )
    return (resid + moe_out.astype(jnp.float32)).astype(jnp.bfloat16)[None]


def solution(mesh):
    return jax.shard_map(
        on_device,
        mesh=mesh,
        in_specs=(
            P("ex", None, None),
            P(),
            P(None, None, "kv"),
            P("kv", None),
            P("ex", None, None, "kv"),
            P("ex"),
            P(),
            P(None, None, "ex", "kv"),
            P("ex", "kv", None),
            P("ex", "kv", None),
        ),
        out_specs=P("ex", "kv", None),
        check_vma=False,
    )
```

```python
import functools
import math

import jax
import jax.numpy as jnp
from jax import lax
from jax.experimental import pallas as pl
from jax.experimental.pallas import tpu as pltpu
from jax.sharding import PartitionSpec as P

HD = 128
TOPK = 8
PLEN = 512
REQ_DEV = 2
QB = 32
CMAX = 512


def rms_scale(rows, gain):
    values = rows.astype(jnp.float32)
    scale = lax.rsqrt(jnp.mean(values * values, axis=-1, keepdims=True) + 1e-06)
    return values * scale * gain


def attention_kernel(scale, len_ref, x_ref, gain_ref, w_ref, cache_ref, w_out_ref, out_ref, normed):
    @pl.when(pl.program_id(0) == 0)
    def _():
        normed[...] = rms_scale(x_ref[...], gain_ref[...]).astype(jnp.bfloat16)
        out_ref[...] = jnp.zeros_like(out_ref)

    rows = normed[...]
    query, keys, values = (
        jnp.dot(rows, w_ref[j], preferred_element_type=jnp.float32).astype(jnp.bfloat16)
        for j in range(3)
    )

    def scores_of(q, k):
        return scale * lax.dot_general(
            q, k, (((1,), (1,)), ((), ())), preferred_element_type=jnp.float32
        )

    def mix(weights, v):
        return jnp.dot(weights.astype(jnp.bfloat16), v, preferred_element_type=jnp.float32)

    heads = []
    for head in range(query.shape[1] // HD):
        cut = slice(head * HD, (head + 1) * HD)
        q, k, v = query[:, cut], keys[:, cut], values[:, cut]
        scores = scores_of(q[:PLEN], k[:PLEN])
        weights = jnp.exp(scores - jnp.max(scores, axis=-1, keepdims=True))
        total = jnp.sum(weights, axis=-1, keepdims=True)
        outs = [(mix(weights, v[:PLEN]) / total).astype(jnp.bfloat16)]
        for request in range(REQ_DEV):
            own = slice(PLEN + request * QB, PLEN + (request + 1) * QB)
            fresh = scores_of(q[own], k[own])
            stored = scores_of(q[own], cache_ref[request, 0, :, cut])
            slots = lax.broadcasted_iota(jnp.int32, stored.shape, 1)
            stored = jnp.where(slots < len_ref[request], stored, -1e30)
            top = jnp.maximum(
                jnp.max(fresh, axis=-1, keepdims=True), jnp.max(stored, axis=-1, keepdims=True)
            )
            fresh, stored = jnp.exp(fresh - top), jnp.exp(stored - top)
            total = jnp.sum(fresh, axis=-1, keepdims=True) + jnp.sum(stored, axis=-1, keepdims=True)
            mixed = mix(fresh, v[own]) + mix(stored, cache_ref[request, 1, :, cut])
            outs.append((mixed / total).astype(jnp.bfloat16))
        heads.append(jnp.concatenate(outs, axis=0))
    out_ref[...] += jnp.dot(
        jnp.concatenate(heads, axis=1), w_out_ref[...], preferred_element_type=jnp.float32
    )


def attention(rows, gain, w_qkv, cache, cache_len, w_out):
    count, width = rows.shape
    units = w_qkv.shape[2]
    block = min(2 * HD, units)
    return pl.pallas_call(
        functools.partial(attention_kernel, 1.0 / math.sqrt(HD)),
        grid=(units // block,),
        in_specs=[
            pl.BlockSpec(memory_space=pltpu.SMEM),
            pl.BlockSpec((count, width), lambda i: (0, 0)),
            pl.BlockSpec((1, width), lambda i: (0, 0)),
            pl.BlockSpec((3, width, block), lambda i: (0, 0, i)),
            pl.BlockSpec((REQ_DEV, 2, CMAX, block), lambda i: (0, 0, 0, i)),
            pl.BlockSpec((block, width), lambda i: (i, 0)),
        ],
        out_specs=pl.BlockSpec((count, width), lambda i: (0, 0)),
        out_shape=jax.ShapeDtypeStruct((count, width), jnp.float32),
        scratch_shapes=[pltpu.VMEM((count, width), jnp.bfloat16)],
        compiler_params=pltpu.CompilerParams(vmem_limit_bytes=38 * 1024 * 1024),
        cost_estimate=pl.CostEstimate(
            flops=8 * count * width * units + 4 * PLEN * PLEN * units,
            bytes_accessed=8 * width * units + 6 * count * width,
            transcendentals=PLEN * PLEN * units // HD,
        ),
        name="attention",
    )(cache_len, rows, gain[None], jnp.transpose(w_qkv, (1, 0, 2)), cache, w_out)


def share_columns(share):
    high = share.astype(jnp.bfloat16)
    low = (share - high.astype(jnp.float32)).astype(jnp.bfloat16)
    spare = -2 * share.shape[1] % 128
    return jnp.concatenate([high, low, jnp.zeros((share.shape[0], spare), jnp.bfloat16)], axis=1)


def hidden_kernel(experts, width, me_ref, *refs):
    x_refs, weight_refs, out_refs = refs[:2], refs[2:-2], refs[-2:]
    units = weight_refs[0].shape[2]
    me = me_ref[0]
    for x_ref, out_ref in zip(x_refs, out_refs):
        extra = x_ref[:, width:].astype(jnp.float32)
        lanes = lax.broadcasted_iota(jnp.int32, extra.shape, 1)
        mine = (lanes == me) | (lanes == me + experts)
        share = jnp.sum(jnp.where(mine, extra, 0.0), axis=-1, keepdims=True)
        for part in range(len(weight_refs) // 2):
            gate_w, up_w = (r[...].reshape(width, units) for r in weight_refs[2 * part : 2 * part + 2])
            x = x_ref[:, :width]
            gate = jnp.dot(x, gate_w, preferred_element_type=jnp.float32)
            up = jnp.dot(x, up_w, preferred_element_type=jnp.float32)
            gate = 0.5 * gate
            out_ref[:, part * units : (part + 1) * units] = (
                (gate + gate * jnp.tanh(gate)) * (up * share)
            ).astype(jnp.bfloat16)


def expert_hidden(experts, me, blocks, weights):
    count = blocks[0].shape[0]
    sources, slice_width, units = weights[0].shape
    width, hidden = sources * slice_width, units * len(weights) // 2
    vmem = pl.BlockSpec(memory_space=pltpu.VMEM)
    out = jax.ShapeDtypeStruct((count, hidden), jnp.bfloat16)
    return pl.pallas_call(
        functools.partial(hidden_kernel, experts, width),
        in_specs=[pl.BlockSpec(memory_space=pltpu.SMEM)] + [vmem] * (2 + len(weights)),
        out_specs=[vmem] * 2,
        out_shape=[out, out],
        compiler_params=pltpu.CompilerParams(vmem_limit_bytes=8 * 1024 * 1024),
        cost_estimate=pl.CostEstimate(
            flops=8 * count * width * hidden,
            bytes_accessed=4 * count * (width + hidden) + 4 * width * hidden,
            transcendentals=2 * count * hidden,
        ),
        name="expert_hidden",
    )(me, *blocks, *weights)


def down_kernel(*refs):
    hidden_refs, weight_refs, out_refs = refs[:2], refs[2:-2], refs[-2:]
    sources, slice_width, units = weight_refs[0].shape
    group = max(1, min(sources, 1024 // slice_width))
    for hidden_ref, out_ref in zip(hidden_refs, out_refs):
        for first in range(0, sources, group):
            total = None
            for part, weight_ref in enumerate(weight_refs):
                term = lax.dot_general(
                    hidden_ref[:, part * units : (part + 1) * units],
                    weight_ref[first : first + group].reshape(group * slice_width, units),
                    (((1,), (1,)), ((), ())),
                    preferred_element_type=jnp.float32,
                )
                total = term if total is None else total + term
            cut = slice(first * slice_width, (first + group) * slice_width)
            out_ref[:, cut] = total.astype(jnp.bfloat16)


def expert_down(hiddens, weights):
    count, hidden = hiddens[0].shape
    width = weights[0].shape[0] * weights[0].shape[1]
    vmem = pl.BlockSpec(memory_space=pltpu.VMEM)
    out = jax.ShapeDtypeStruct((count, width), jnp.bfloat16)
    return pl.pallas_call(
        down_kernel,
        in_specs=[vmem] * (2 + len(weights)),
        out_specs=[vmem] * 2,
        out_shape=[out, out],
        compiler_params=pltpu.CompilerParams(vmem_limit_bytes=8 * 1024 * 1024),
        cost_estimate=pl.CostEstimate(
            flops=4 * count * width * hidden,
            bytes_accessed=4 * count * (width + hidden) + 2 * width * hidden,
            transcendentals=0,
        ),
        name="expert_down",
    )(*hiddens, *weights)


def sum_kernel(cut, refs):
    total = refs[0][:, cut].astype(jnp.float32) + refs[1][:, cut].astype(jnp.float32)
    for ref in refs[2:-1]:
        total = total + ref[...].astype(jnp.float32)
    refs[-1][...] = total.astype(jnp.bfloat16)


def add_terms(cut, keep, got, running):
    terms = [keep, got] + ([] if running is None else [running])
    columns = cut.stop - cut.start
    vmem = pl.BlockSpec(memory_space=pltpu.VMEM)
    return pl.pallas_call(
        lambda *refs: sum_kernel(cut, refs),
        in_specs=[vmem] * len(terms),
        out_specs=vmem,
        out_shape=jax.ShapeDtypeStruct((keep.shape[0], columns), jnp.bfloat16),
        compiler_params=pltpu.CompilerParams(vmem_limit_bytes=8 * 1024 * 1024),
        cost_estimate=pl.CostEstimate(
            flops=2 * keep.shape[0] * columns,
            bytes_accessed=8 * keep.shape[0] * columns,
            transcendentals=0,
        ),
        name="add_terms",
    )(*terms)


def chip_ring(chips):
    rows = 4
    columns = chips // rows
    if chips % rows or columns < 2:
        return list(range(chips))
    order = [z * columns for z in range(rows)]
    for turn, z in enumerate(reversed(range(rows))):
        line = [z * columns + x for x in range(1, columns)]
        order += line if turn % 2 == 0 else line[::-1]
    return order


def on_device(
    x_tokens,
    attn_gain,
    w_qkv,
    w_out,
    cache,
    cache_len,
    moe_gain,
    w_trainer,
    expert_ids,
    route_probs,
):
    kv, ex = lax.axis_size("kv"), lax.axis_size("ex")
    me, me_kv = lax.axis_index("ex"), lax.axis_index("kv")
    experts = w_trainer.shape[0]

    def over_experts(part):
        return lax.all_to_all(part, "ex", split_axis=0, concat_axis=0, tiled=True)

    def over_kv(part):
        return [
            lax.ppermute(part, "kv", [(i, (i + turn) % kv) for i in range(kv)])
            for turn in range(1, kv)
        ]

    probs = route_probs[0]
    share = probs / jnp.sum(probs, axis=-1, keepdims=True)
    named = expert_ids[0][:, :, None] == jnp.arange(experts, dtype=jnp.int32)[None, None, :]
    factor = jnp.sum(jnp.where(named, share[:, :, None], 0.0), axis=1)
    factor = share_columns(factor)

    rows = x_tokens[0]
    row_count = rows.shape[0]
    rows_dev = row_count // kv
    gate = w_trainer[:, 0].astype(jnp.bfloat16)
    gate, rest = lax.optimization_barrier((gate, w_trainer))
    up, down = (rest[:, kind].astype(jnp.bfloat16) for kind in (1, 2))
    gate = over_experts(gate)
    mixed = attention(rows, attn_gain, w_qkv, cache, cache_len, w_out)
    mixed, gate, up, down = lax.optimization_barrier((mixed, gate, up, down))
    gates = over_kv(gate)
    up = over_experts(up)
    mixed = mixed.reshape(kv, rows_dev, mixed.shape[1])

    def rows_of(part):
        return lax.dynamic_index_in_dim(mixed, part, 0, keepdims=False)

    own_rows = lax.dynamic_slice_in_dim(rows, me_kv * rows_dev, rows_dev, 0)
    resid = own_rows.astype(jnp.float32) + rows_of(me_kv)
    for turn in range(1, kv):
        sent = rows_of(lax.rem(me_kv + turn, kv)).astype(jnp.bfloat16)
        sent = lax.ppermute(sent, "kv", [(i, (i + turn) % kv) for i in range(kv)])
        resid = resid + sent.astype(jnp.float32)
    resid, up, down = lax.optimization_barrier((resid, up, down))
    ups = over_kv(up)
    down = over_experts(down)
    moe_in = rms_scale(resid, moe_gain).astype(jnp.bfloat16)
    moe_in = jnp.concatenate([moe_in, factor], axis=1)

    cores = 2
    order = chip_ring(ex // cores)
    chips = len(order)
    half = rows_dev // 2
    core = lax.rem(me, cores)
    ring, swap = [], [(i, i ^ 1) for i in range(ex)]
    for spot, chip in enumerate(order):
        for c in range(cores):
            here = chip * cores + c
            ring.append((here, order[(spot + 1 - 2 * c) % chips] * cores + c))

    def half_of(array, which):
        return lax.dynamic_slice_in_dim(array, which * half, half, 0)

    got = lax.ppermute(half_of(moe_in, 1 - core), "ex", swap)
    held = jnp.concatenate([half_of(moe_in, core), got], axis=0)
    first_weights = [gate, up]
    due = {2: [0], 3: [1, 2], 4: [3], 5: [4], 6: [5], 7: [6]}
    held, gates, down = lax.optimization_barrier((held, gates, down))
    downs = over_kv(down)
    blocks, hiddens = [held], {}

    def hidden_of(step):
        other = lax.ppermute(blocks[step], "ex", swap)
        return expert_hidden(experts, me[None], [blocks[step], other], first_weights)

    for step in range(1, chips):
        held = lax.ppermute(held, "ex", ring)
        if step == 1:
            held, ups = lax.optimization_barrier((held, ups))
            for pair in zip(gates, ups):
                first_weights += pair
        blocks.append(held)
        for early in due.get(step, []):
            hiddens[early] = hidden_of(early)
            held, hiddens[early] = lax.optimization_barrier((held, hiddens[early]))
        if step == min(3, chips - 1):
            held, downs = lax.optimization_barrier((held, downs))
        blocks[step] = held
    for step in range(chips):
        if step not in hiddens:
            hiddens[step] = hidden_of(step)
    hiddens = [hiddens[step] for step in range(chips)]
    keeps, gots = [], []
    for pair in hiddens:
        keep, give = expert_down(pair, [down] + downs)
        keeps.append(keep)
        gots.append(lax.ppermute(give, "ex", swap))

    width = w_out.shape[1]
    sums = []
    for cut in (slice(0, width // 2), slice(width // 2, width)):
        running = None
        for step in list(range(1, chips)) + [0]:
            running = add_terms(cut, keeps[step], gots[step], running)
            if step:
                running = lax.ppermute(running, "ex", ring)
        sums.append(running)
    running = jnp.concatenate(sums, axis=1)
    got = lax.ppermute(running[half:], "ex", swap)
    moe_out = jnp.where(
        core == 0,
        jnp.concatenate([running[:half], got], axis=0),
        jnp.concatenate([got, running[:half]], axis=0),
    )
    return (resid + moe_out.astype(jnp.float32)).astype(jnp.bfloat16)[None]


def solution(mesh):
    return jax.shard_map(
        on_device,
        mesh=mesh,
        in_specs=(
            P("ex", None, None),
            P(),
            P(None, None, "kv"),
            P("kv", None),
            P("ex", None, None, "kv"),
            P("ex"),
            P(),
            P(None, None, "ex", "kv"),
            P("ex", "kv", None),
            P("ex", "kv", None),
        ),
        out_specs=P("ex", "kv", None),
        check_vma=False,
    )
```

```python
import functools
import math

import jax
import jax.numpy as jnp
from jax import lax
from jax.experimental import pallas as pl
from jax.experimental.pallas import tpu as pltpu
from jax.sharding import PartitionSpec as P

HD = 128
TOPK = 8
PLEN = 512
REQ_DEV = 2
QB = 32
CMAX = 512


def rms_scale(rows, gain):
    values = rows.astype(jnp.float32)
    scale = lax.rsqrt(jnp.mean(values * values, axis=-1, keepdims=True) + 1e-06)
    return values * scale * gain


def attention_kernel(scale, len_ref, x_ref, gain_ref, w_ref, cache_ref, w_out_ref, out_ref, normed):
    @pl.when(pl.program_id(0) == 0)
    def _():
        normed[...] = rms_scale(x_ref[...], gain_ref[...]).astype(jnp.bfloat16)
        out_ref[...] = jnp.zeros_like(out_ref)

    rows = normed[...]
    query, keys, values = (
        jnp.dot(rows, w_ref[j], preferred_element_type=jnp.float32).astype(jnp.bfloat16)
        for j in range(3)
    )

    def scores_of(q, k):
        return scale * lax.dot_general(
            q, k, (((1,), (1,)), ((), ())), preferred_element_type=jnp.float32
        )

    def mix(weights, v):
        return jnp.dot(weights.astype(jnp.bfloat16), v, preferred_element_type=jnp.float32)

    heads = []
    for head in range(query.shape[1] // HD):
        cut = slice(head * HD, (head + 1) * HD)
        q, k, v = query[:, cut], keys[:, cut], values[:, cut]
        scores = scores_of(q[:PLEN], k[:PLEN])
        weights = jnp.exp(scores - jnp.max(scores, axis=-1, keepdims=True))
        total = jnp.sum(weights, axis=-1, keepdims=True)
        outs = [(mix(weights, v[:PLEN]) / total).astype(jnp.bfloat16)]
        for request in range(REQ_DEV):
            own = slice(PLEN + request * QB, PLEN + (request + 1) * QB)
            fresh = scores_of(q[own], k[own])
            stored = scores_of(q[own], cache_ref[request, 0, :, cut])
            slots = lax.broadcasted_iota(jnp.int32, stored.shape, 1)
            stored = jnp.where(slots < len_ref[request], stored, -1e30)
            top = jnp.maximum(
                jnp.max(fresh, axis=-1, keepdims=True), jnp.max(stored, axis=-1, keepdims=True)
            )
            fresh, stored = jnp.exp(fresh - top), jnp.exp(stored - top)
            total = jnp.sum(fresh, axis=-1, keepdims=True) + jnp.sum(stored, axis=-1, keepdims=True)
            mixed = mix(fresh, v[own]) + mix(stored, cache_ref[request, 1, :, cut])
            outs.append((mixed / total).astype(jnp.bfloat16))
        heads.append(jnp.concatenate(outs, axis=0))
    out_ref[...] += jnp.dot(
        jnp.concatenate(heads, axis=1), w_out_ref[...], preferred_element_type=jnp.float32
    )


def attention(rows, gain, w_qkv, cache, cache_len, w_out):
    count, width = rows.shape
    units = w_qkv.shape[2]
    block = min(2 * HD, units)
    return pl.pallas_call(
        functools.partial(attention_kernel, 1.0 / math.sqrt(HD)),
        grid=(units // block,),
        in_specs=[
            pl.BlockSpec(memory_space=pltpu.SMEM),
            pl.BlockSpec((count, width), lambda i: (0, 0)),
            pl.BlockSpec((1, width), lambda i: (0, 0)),
            pl.BlockSpec((3, width, block), lambda i: (0, 0, i)),
            pl.BlockSpec((REQ_DEV, 2, CMAX, block), lambda i: (0, 0, 0, i)),
            pl.BlockSpec((block, width), lambda i: (i, 0)),
        ],
        out_specs=pl.BlockSpec((count, width), lambda i: (0, 0)),
        out_shape=jax.ShapeDtypeStruct((count, width), jnp.float32),
        scratch_shapes=[pltpu.VMEM((count, width), jnp.bfloat16)],
        compiler_params=pltpu.CompilerParams(vmem_limit_bytes=38 * 1024 * 1024),
        cost_estimate=pl.CostEstimate(
            flops=8 * count * width * units + 4 * PLEN * PLEN * units,
            bytes_accessed=8 * width * units + 6 * count * width,
            transcendentals=PLEN * PLEN * units // HD,
        ),
        name="attention",
    )(cache_len, rows, gain[None], jnp.transpose(w_qkv, (1, 0, 2)), cache, w_out)


def share_columns(share):
    high = share.astype(jnp.bfloat16)
    low = (share - high.astype(jnp.float32)).astype(jnp.bfloat16)
    spare = -2 * share.shape[1] % 128
    return jnp.concatenate([high, low, jnp.zeros((share.shape[0], spare), jnp.bfloat16)], axis=1)


def hidden_kernel(experts, width, me_ref, *refs):
    x_refs, weight_refs, out_refs = refs[:2], refs[2:-2], refs[-2:]
    units = weight_refs[0].shape[2]
    me = me_ref[0]
    for x_ref, out_ref in zip(x_refs, out_refs):
        extra = x_ref[:, width:].astype(jnp.float32)
        lanes = lax.broadcasted_iota(jnp.int32, extra.shape, 1)
        mine = (lanes == me) | (lanes == me + experts)
        share = jnp.sum(jnp.where(mine, extra, 0.0), axis=-1, keepdims=True)
        for part in range(len(weight_refs) // 2):
            gate_w, up_w = (r[...].reshape(width, units) for r in weight_refs[2 * part : 2 * part + 2])
            x = x_ref[:, :width]
            gate = jnp.dot(x, gate_w, preferred_element_type=jnp.float32)
            up = jnp.dot(x, up_w, preferred_element_type=jnp.float32)
            gate = 0.5 * gate
            out_ref[:, part * units : (part + 1) * units] = (
                (gate + gate * jnp.tanh(gate)) * (up * share)
            ).astype(jnp.bfloat16)


def expert_hidden(experts, me, blocks, weights):
    count = blocks[0].shape[0]
    sources, slice_width, units = weights[0].shape
    width, hidden = sources * slice_width, units * len(weights) // 2
    vmem = pl.BlockSpec(memory_space=pltpu.VMEM)
    out = jax.ShapeDtypeStruct((count, hidden), jnp.bfloat16)
    return pl.pallas_call(
        functools.partial(hidden_kernel, experts, width),
        in_specs=[pl.BlockSpec(memory_space=pltpu.SMEM)] + [vmem] * (2 + len(weights)),
        out_specs=[vmem] * 2,
        out_shape=[out, out],
        compiler_params=pltpu.CompilerParams(vmem_limit_bytes=8 * 1024 * 1024),
        cost_estimate=pl.CostEstimate(
            flops=8 * count * width * hidden,
            bytes_accessed=4 * count * (width + hidden) + 4 * width * hidden,
            transcendentals=2 * count * hidden,
        ),
        name="expert_hidden",
    )(me, *blocks, *weights)


def down_kernel(*refs):
    hidden_refs, weight_refs, out_refs = refs[:2], refs[2:-2], refs[-2:]
    sources, slice_width, units = weight_refs[0].shape
    group = max(1, min(sources, 1024 // slice_width))
    for hidden_ref, out_ref in zip(hidden_refs, out_refs):
        for first in range(0, sources, group):
            total = None
            for part, weight_ref in enumerate(weight_refs):
                term = lax.dot_general(
                    hidden_ref[:, part * units : (part + 1) * units],
                    weight_ref[first : first + group].reshape(group * slice_width, units),
                    (((1,), (1,)), ((), ())),
                    preferred_element_type=jnp.float32,
                )
                total = term if total is None else total + term
            cut = slice(first * slice_width, (first + group) * slice_width)
            out_ref[:, cut] = total.astype(jnp.bfloat16)


def expert_down(hiddens, weights):
    count, hidden = hiddens[0].shape
    width = weights[0].shape[0] * weights[0].shape[1]
    vmem = pl.BlockSpec(memory_space=pltpu.VMEM)
    out = jax.ShapeDtypeStruct((count, width), jnp.bfloat16)
    return pl.pallas_call(
        down_kernel,
        in_specs=[vmem] * (2 + len(weights)),
        out_specs=[vmem] * 2,
        out_shape=[out, out],
        compiler_params=pltpu.CompilerParams(vmem_limit_bytes=8 * 1024 * 1024),
        cost_estimate=pl.CostEstimate(
            flops=4 * count * width * hidden,
            bytes_accessed=4 * count * (width + hidden) + 2 * width * hidden,
            transcendentals=0,
        ),
        name="expert_down",
    )(*hiddens, *weights)


def sum_kernel(cut, refs):
    total = refs[0][:, cut].astype(jnp.float32) + refs[1][:, cut].astype(jnp.float32)
    for ref in refs[2:-1]:
        total = total + ref[...].astype(jnp.float32)
    refs[-1][...] = total.astype(jnp.bfloat16)


def add_terms(cut, keep, got, running):
    terms = [keep, got] + ([] if running is None else [running])
    columns = cut.stop - cut.start
    vmem = pl.BlockSpec(memory_space=pltpu.VMEM)
    return pl.pallas_call(
        lambda *refs: sum_kernel(cut, refs),
        in_specs=[vmem] * len(terms),
        out_specs=vmem,
        out_shape=jax.ShapeDtypeStruct((keep.shape[0], columns), jnp.bfloat16),
        compiler_params=pltpu.CompilerParams(vmem_limit_bytes=8 * 1024 * 1024),
        cost_estimate=pl.CostEstimate(
            flops=2 * keep.shape[0] * columns,
            bytes_accessed=8 * keep.shape[0] * columns,
            transcendentals=0,
        ),
        name="add_terms",
    )(*terms)


def chip_ring(chips):
    rows = 4
    columns = chips // rows
    if chips % rows or columns < 2:
        return list(range(chips))
    order = [z * columns for z in range(rows)]
    for turn, z in enumerate(reversed(range(rows))):
        line = [z * columns + x for x in range(1, columns)]
        order += line if turn % 2 == 0 else line[::-1]
    return order


def on_device(
    x_tokens,
    attn_gain,
    w_qkv,
    w_out,
    cache,
    cache_len,
    moe_gain,
    w_trainer,
    expert_ids,
    route_probs,
):
    kv, ex = lax.axis_size("kv"), lax.axis_size("ex")
    me, me_kv = lax.axis_index("ex"), lax.axis_index("kv")
    experts = w_trainer.shape[0]

    def over_experts(part):
        return lax.all_to_all(part, "ex", split_axis=0, concat_axis=0, tiled=True)

    def over_kv(part):
        return [
            lax.ppermute(part, "kv", [(i, (i + turn) % kv) for i in range(kv)])
            for turn in range(1, kv)
        ]

    probs = route_probs[0]
    share = probs / jnp.sum(probs, axis=-1, keepdims=True)
    named = expert_ids[0][:, :, None] == jnp.arange(experts, dtype=jnp.int32)[None, None, :]
    factor = jnp.sum(jnp.where(named, share[:, :, None], 0.0), axis=1)
    factor = share_columns(factor)

    rows = x_tokens[0]
    row_count = rows.shape[0]
    rows_dev = row_count // kv
    gate = w_trainer[:, 0].astype(jnp.bfloat16)
    gate, rest = lax.optimization_barrier((gate, w_trainer))
    up, down = (rest[:, kind].astype(jnp.bfloat16) for kind in (1, 2))
    gate = over_experts(gate)
    mixed = attention(rows, attn_gain, w_qkv, cache, cache_len, w_out)
    mixed, gate, up, down = lax.optimization_barrier((mixed, gate, up, down))
    gates = over_kv(gate)
    up = over_experts(up)
    mixed = mixed.reshape(kv, rows_dev, mixed.shape[1])

    def rows_of(part):
        return lax.dynamic_index_in_dim(mixed, part, 0, keepdims=False)

    own_rows = lax.dynamic_slice_in_dim(rows, me_kv * rows_dev, rows_dev, 0)
    resid = own_rows.astype(jnp.float32) + rows_of(me_kv)
    for turn in range(1, kv):
        sent = rows_of(lax.rem(me_kv + turn, kv)).astype(jnp.bfloat16)
        sent = lax.ppermute(sent, "kv", [(i, (i + turn) % kv) for i in range(kv)])
        resid = resid + sent.astype(jnp.float32)
    resid, up, down = lax.optimization_barrier((resid, up, down))
    ups = over_kv(up)
    down = over_experts(down)
    moe_in = rms_scale(resid, moe_gain).astype(jnp.bfloat16)
    moe_in = jnp.concatenate([moe_in, factor], axis=1)

    cores = 2
    order = chip_ring(ex // cores)
    chips = len(order)
    half = rows_dev // 2
    core = lax.rem(me, cores)
    ring, swap = [], [(i, i ^ 1) for i in range(ex)]
    for spot, chip in enumerate(order):
        for c in range(cores):
            here = chip * cores + c
            ring.append((here, order[(spot + 1 - 2 * c) % chips] * cores + c))

    def half_of(array, which):
        return lax.dynamic_slice_in_dim(array, which * half, half, 0)

    got = lax.ppermute(half_of(moe_in, 1 - core), "ex", swap)
    held = jnp.concatenate([half_of(moe_in, core), got], axis=0)
    first_weights = [gate, up]
    due = {3: [0, 1], 4: [2, 3], 5: [4], 6: [5], 7: [6]}
    held, gates = lax.optimization_barrier((held, gates))
    blocks, hiddens = [held], {}

    def hidden_of(step):
        other = lax.ppermute(blocks[step], "ex", swap)
        return expert_hidden(experts, me[None], [blocks[step], other], first_weights)

    for step in range(1, chips):
        held = lax.ppermute(held, "ex", ring)
        if step == 1:
            held, down = lax.optimization_barrier((held, down))
            downs = over_kv(down)
        if step == 2:
            held, ups = lax.optimization_barrier((held, ups))
            for pair in zip(gates, ups):
                first_weights += pair
        blocks.append(held)
        for early in due.get(step, []):
            hiddens[early] = hidden_of(early)
            held, hiddens[early] = lax.optimization_barrier((held, hiddens[early]))
        if step == min(3, chips - 1):
            held, downs = lax.optimization_barrier((held, downs))
        blocks[step] = held
    for step in range(chips):
        if step not in hiddens:
            hiddens[step] = hidden_of(step)
    hiddens = [hiddens[step] for step in range(chips)]
    keeps, gots = [], []
    for pair in hiddens:
        keep, give = expert_down(pair, [down] + downs)
        keeps.append(keep)
        gots.append(lax.ppermute(give, "ex", swap))

    width = w_out.shape[1]
    sums = []
    for cut in (slice(0, width // 2), slice(width // 2, width)):
        running = None
        for step in list(range(1, chips)) + [0]:
            running = add_terms(cut, keeps[step], gots[step], running)
            if step:
                running = lax.ppermute(running, "ex", ring)
        sums.append(running)
    running = jnp.concatenate(sums, axis=1)
    got = lax.ppermute(running[half:], "ex", swap)
    moe_out = jnp.where(
        core == 0,
        jnp.concatenate([running[:half], got], axis=0),
        jnp.concatenate([got, running[:half]], axis=0),
    )
    return (resid + moe_out.astype(jnp.float32)).astype(jnp.bfloat16)[None]


def solution(mesh):
    return jax.shard_map(
        on_device,
        mesh=mesh,
        in_specs=(
            P("ex", None, None),
            P(),
            P(None, None, "kv"),
            P("kv", None),
            P("ex", None, None, "kv"),
            P("ex"),
            P(),
            P(None, None, "ex", "kv"),
            P("ex", "kv", None),
            P("ex", "kv", None),
        ),
        out_specs=P("ex", "kv", None),
        check_vma=False,
    )
```

```python
import functools
import math

import jax
import jax.numpy as jnp
from jax import lax
from jax.experimental import pallas as pl
from jax.experimental.pallas import tpu as pltpu
from jax.sharding import PartitionSpec as P

HD = 128
TOPK = 8
PLEN = 512
REQ_DEV = 2
QB = 32
CMAX = 512


def rms_scale(rows, gain):
    values = rows.astype(jnp.float32)
    scale = lax.rsqrt(jnp.mean(values * values, axis=-1, keepdims=True) + 1e-06)
    return values * scale * gain


def attention_kernel(scale, len_ref, x_ref, gain_ref, w_ref, cache_ref, w_out_ref, out_ref, normed):
    @pl.when(pl.program_id(0) == 0)
    def _():
        normed[...] = rms_scale(x_ref[...], gain_ref[...]).astype(jnp.bfloat16)
        out_ref[...] = jnp.zeros_like(out_ref)

    rows = normed[...]
    query, keys, values = (
        jnp.dot(rows, w_ref[j], preferred_element_type=jnp.float32).astype(jnp.bfloat16)
        for j in range(3)
    )

    def scores_of(q, k):
        return scale * lax.dot_general(
            q, k, (((1,), (1,)), ((), ())), preferred_element_type=jnp.float32
        )

    def mix(weights, v):
        return jnp.dot(weights.astype(jnp.bfloat16), v, preferred_element_type=jnp.float32)

    heads = []
    for head in range(query.shape[1] // HD):
        cut = slice(head * HD, (head + 1) * HD)
        q, k, v = query[:, cut], keys[:, cut], values[:, cut]
        scores = scores_of(q[:PLEN], k[:PLEN])
        weights = jnp.exp(scores - jnp.max(scores, axis=-1, keepdims=True))
        total = jnp.sum(weights, axis=-1, keepdims=True)
        outs = [(mix(weights, v[:PLEN]) / total).astype(jnp.bfloat16)]
        for request in range(REQ_DEV):
            own = slice(PLEN + request * QB, PLEN + (request + 1) * QB)
            fresh = scores_of(q[own], k[own])
            stored = scores_of(q[own], cache_ref[request, 0, :, cut])
            slots = lax.broadcasted_iota(jnp.int32, stored.shape, 1)
            stored = jnp.where(slots < len_ref[request], stored, -1e30)
            top = jnp.maximum(
                jnp.max(fresh, axis=-1, keepdims=True), jnp.max(stored, axis=-1, keepdims=True)
            )
            fresh, stored = jnp.exp(fresh - top), jnp.exp(stored - top)
            total = jnp.sum(fresh, axis=-1, keepdims=True) + jnp.sum(stored, axis=-1, keepdims=True)
            mixed = mix(fresh, v[own]) + mix(stored, cache_ref[request, 1, :, cut])
            outs.append((mixed / total).astype(jnp.bfloat16))
        heads.append(jnp.concatenate(outs, axis=0))
    out_ref[...] += jnp.dot(
        jnp.concatenate(heads, axis=1), w_out_ref[...], preferred_element_type=jnp.float32
    )


def attention(rows, gain, w_qkv, cache, cache_len, w_out):
    count, width = rows.shape
    units = w_qkv.shape[2]
    block = min(2 * HD, units)
    return pl.pallas_call(
        functools.partial(attention_kernel, 1.0 / math.sqrt(HD)),
        grid=(units // block,),
        in_specs=[
            pl.BlockSpec(memory_space=pltpu.SMEM),
            pl.BlockSpec((count, width), lambda i: (0, 0)),
            pl.BlockSpec((1, width), lambda i: (0, 0)),
            pl.BlockSpec((3, width, block), lambda i: (0, 0, i)),
            pl.BlockSpec((REQ_DEV, 2, CMAX, block), lambda i: (0, 0, 0, i)),
            pl.BlockSpec((block, width), lambda i: (i, 0)),
        ],
        out_specs=pl.BlockSpec((count, width), lambda i: (0, 0)),
        out_shape=jax.ShapeDtypeStruct((count, width), jnp.float32),
        scratch_shapes=[pltpu.VMEM((count, width), jnp.bfloat16)],
        compiler_params=pltpu.CompilerParams(vmem_limit_bytes=38 * 1024 * 1024),
        cost_estimate=pl.CostEstimate(
            flops=8 * count * width * units + 4 * PLEN * PLEN * units,
            bytes_accessed=8 * width * units + 6 * count * width,
            transcendentals=PLEN * PLEN * units // HD,
        ),
        name="attention",
    )(cache_len, rows, gain[None], jnp.transpose(w_qkv, (1, 0, 2)), cache, w_out)


def share_columns(share):
    high = share.astype(jnp.bfloat16)
    low = (share - high.astype(jnp.float32)).astype(jnp.bfloat16)
    spare = -2 * share.shape[1] % 128
    return jnp.concatenate([high, low, jnp.zeros((share.shape[0], spare), jnp.bfloat16)], axis=1)


def hidden_kernel(experts, width, me_ref, *refs):
    x_refs, weight_refs, out_refs = refs[:2], refs[2:-2], refs[-2:]
    units = weight_refs[0].shape[2]
    me = me_ref[0]
    for x_ref, out_ref in zip(x_refs, out_refs):
        extra = x_ref[:, width:].astype(jnp.float32)
        lanes = lax.broadcasted_iota(jnp.int32, extra.shape, 1)
        mine = (lanes == me) | (lanes == me + experts)
        share = jnp.sum(jnp.where(mine, extra, 0.0), axis=-1, keepdims=True)
        for part in range(len(weight_refs) // 2):
            gate_w, up_w = (r[...].reshape(width, units) for r in weight_refs[2 * part : 2 * part + 2])
            x = x_ref[:, :width]
            gate = jnp.dot(x, gate_w, preferred_element_type=jnp.float32)
            up = jnp.dot(x, up_w, preferred_element_type=jnp.float32)
            gate = 0.5 * gate
            out_ref[:, part * units : (part + 1) * units] = (
                (gate + gate * jnp.tanh(gate)) * (up * share)
            ).astype(jnp.bfloat16)


def expert_hidden(experts, me, blocks, weights):
    count = blocks[0].shape[0]
    sources, slice_width, units = weights[0].shape
    width, hidden = sources * slice_width, units * len(weights) // 2
    vmem = pl.BlockSpec(memory_space=pltpu.VMEM)
    out = jax.ShapeDtypeStruct((count, hidden), jnp.bfloat16)
    return pl.pallas_call(
        functools.partial(hidden_kernel, experts, width),
        in_specs=[pl.BlockSpec(memory_space=pltpu.SMEM)] + [vmem] * (2 + len(weights)),
        out_specs=[vmem] * 2,
        out_shape=[out, out],
        compiler_params=pltpu.CompilerParams(vmem_limit_bytes=8 * 1024 * 1024),
        cost_estimate=pl.CostEstimate(
            flops=8 * count * width * hidden,
            bytes_accessed=4 * count * (width + hidden) + 4 * width * hidden,
            transcendentals=2 * count * hidden,
        ),
        name="expert_hidden",
    )(me, *blocks, *weights)


def down_kernel(*refs):
    hidden_refs, weight_refs, out_refs = refs[:2], refs[2:-2], refs[-2:]
    sources, slice_width, units = weight_refs[0].shape
    group = max(1, min(sources, 1024 // slice_width))
    for hidden_ref, out_ref in zip(hidden_refs, out_refs):
        for first in range(0, sources, group):
            total = None
            for part, weight_ref in enumerate(weight_refs):
                term = lax.dot_general(
                    hidden_ref[:, part * units : (part + 1) * units],
                    weight_ref[first : first + group].reshape(group * slice_width, units),
                    (((1,), (1,)), ((), ())),
                    preferred_element_type=jnp.float32,
                )
                total = term if total is None else total + term
            cut = slice(first * slice_width, (first + group) * slice_width)
            out_ref[:, cut] = total.astype(jnp.bfloat16)


def expert_down(hiddens, weights):
    count, hidden = hiddens[0].shape
    width = weights[0].shape[0] * weights[0].shape[1]
    vmem = pl.BlockSpec(memory_space=pltpu.VMEM)
    out = jax.ShapeDtypeStruct((count, width), jnp.bfloat16)
    return pl.pallas_call(
        down_kernel,
        in_specs=[vmem] * (2 + len(weights)),
        out_specs=[vmem] * 2,
        out_shape=[out, out],
        compiler_params=pltpu.CompilerParams(vmem_limit_bytes=8 * 1024 * 1024),
        cost_estimate=pl.CostEstimate(
            flops=4 * count * width * hidden,
            bytes_accessed=4 * count * (width + hidden) + 2 * width * hidden,
            transcendentals=0,
        ),
        name="expert_down",
    )(*hiddens, *weights)


def sum_kernel(cut, refs):
    total = refs[0][:, cut].astype(jnp.float32) + refs[1][:, cut].astype(jnp.float32)
    for ref in refs[2:-1]:
        total = total + ref[...].astype(jnp.float32)
    refs[-1][...] = total.astype(jnp.bfloat16)


def add_terms(cut, keep, got, running):
    terms = [keep, got] + ([] if running is None else [running])
    columns = cut.stop - cut.start
    vmem = pl.BlockSpec(memory_space=pltpu.VMEM)
    return pl.pallas_call(
        lambda *refs: sum_kernel(cut, refs),
        in_specs=[vmem] * len(terms),
        out_specs=vmem,
        out_shape=jax.ShapeDtypeStruct((keep.shape[0], columns), jnp.bfloat16),
        compiler_params=pltpu.CompilerParams(vmem_limit_bytes=8 * 1024 * 1024),
        cost_estimate=pl.CostEstimate(
            flops=2 * keep.shape[0] * columns,
            bytes_accessed=8 * keep.shape[0] * columns,
            transcendentals=0,
        ),
        name="add_terms",
    )(*terms)


def chip_ring(chips):
    rows = 4
    columns = chips // rows
    if chips % rows or columns < 2:
        return list(range(chips))
    order = [z * columns for z in range(rows)]
    for turn, z in enumerate(reversed(range(rows))):
        line = [z * columns + x for x in range(1, columns)]
        order += line if turn % 2 == 0 else line[::-1]
    return order


def on_device(
    x_tokens,
    attn_gain,
    w_qkv,
    w_out,
    cache,
    cache_len,
    moe_gain,
    w_trainer,
    expert_ids,
    route_probs,
):
    kv, ex = lax.axis_size("kv"), lax.axis_size("ex")
    me, me_kv = lax.axis_index("ex"), lax.axis_index("kv")
    experts = w_trainer.shape[0]

    def over_experts(part):
        return lax.all_to_all(part, "ex", split_axis=0, concat_axis=0, tiled=True)

    def over_kv(part):
        return [
            lax.ppermute(part, "kv", [(i, (i + turn) % kv) for i in range(kv)])
            for turn in range(1, kv)
        ]

    probs = route_probs[0]
    share = probs / jnp.sum(probs, axis=-1, keepdims=True)
    named = expert_ids[0][:, :, None] == jnp.arange(experts, dtype=jnp.int32)[None, None, :]
    factor = jnp.sum(jnp.where(named, share[:, :, None], 0.0), axis=1)
    factor = share_columns(factor)

    rows = x_tokens[0]
    row_count = rows.shape[0]
    rows_dev = row_count // kv
    gate = w_trainer[:, 0].astype(jnp.bfloat16)
    gate, rest = lax.optimization_barrier((gate, w_trainer))
    up, down = (rest[:, kind].astype(jnp.bfloat16) for kind in (1, 2))
    gate = over_experts(gate)
    mixed = attention(rows, attn_gain, w_qkv, cache, cache_len, w_out)
    mixed, gate, up, down = lax.optimization_barrier((mixed, gate, up, down))
    gates = over_kv(gate)
    up = over_experts(up)
    mixed = mixed.reshape(kv, rows_dev, mixed.shape[1])

    def rows_of(part):
        return lax.dynamic_index_in_dim(mixed, part, 0, keepdims=False)

    own_rows = lax.dynamic_slice_in_dim(rows, me_kv * rows_dev, rows_dev, 0)
    resid = own_rows.astype(jnp.float32) + rows_of(me_kv)
    for turn in range(1, kv):
        sent = rows_of(lax.rem(me_kv + turn, kv)).astype(jnp.bfloat16)
        sent = lax.ppermute(sent, "kv", [(i, (i + turn) % kv) for i in range(kv)])
        resid = resid + sent.astype(jnp.float32)
    resid, up, down = lax.optimization_barrier((resid, up, down))
    ups = over_kv(up)
    down = over_experts(down)
    moe_in = rms_scale(resid, moe_gain).astype(jnp.bfloat16)
    moe_in = jnp.concatenate([moe_in, factor], axis=1)
    moe_in, gates = lax.optimization_barrier((moe_in, gates))

    cores = 2
    order = chip_ring(ex // cores)
    chips = len(order)
    half = rows_dev // 2
    core = lax.rem(me, cores)
    ring, swap = [], [(i, i ^ 1) for i in range(ex)]
    for spot, chip in enumerate(order):
        for c in range(cores):
            here = chip * cores + c
            ring.append((here, order[(spot + 1 - 2 * c) % chips] * cores + c))

    def half_of(array, which):
        return lax.dynamic_slice_in_dim(array, which * half, half, 0)

    got = lax.ppermute(half_of(moe_in, 1 - core), "ex", swap)
    held = jnp.concatenate([half_of(moe_in, core), got], axis=0)
    first_weights = [gate, up]
    due = {3: [0, 1], 4: [2, 3], 5: [4], 6: [5], 7: [6]}
    blocks, hiddens = [held], {}

    def hidden_of(step):
        other = lax.ppermute(blocks[step], "ex", swap)
        return expert_hidden(experts, me[None], [blocks[step], other], first_weights)

    for step in range(1, chips):
        held = lax.ppermute(held, "ex", ring)
        if step == 1:
            held, down = lax.optimization_barrier((held, down))
            downs = over_kv(down)
        if step == 2:
            held, ups = lax.optimization_barrier((held, ups))
            for pair in zip(gates, ups):
                first_weights += pair
        blocks.append(held)
        for early in due.get(step, []):
            hiddens[early] = hidden_of(early)
            held, hiddens[early] = lax.optimization_barrier((held, hiddens[early]))
        if step == min(3, chips - 1):
            held, downs = lax.optimization_barrier((held, downs))
        blocks[step] = held
    for step in range(chips):
        if step not in hiddens:
            hiddens[step] = hidden_of(step)
    hiddens = [hiddens[step] for step in range(chips)]
    keeps, gots = [], []
    for pair in hiddens:
        keep, give = expert_down(pair, [down] + downs)
        keeps.append(keep)
        gots.append(lax.ppermute(give, "ex", swap))

    width = w_out.shape[1]
    sums = []
    for cut in (slice(0, width // 2), slice(width // 2, width)):
        running = None
        for step in list(range(1, chips)) + [0]:
            running = add_terms(cut, keeps[step], gots[step], running)
            if step:
                running = lax.ppermute(running, "ex", ring)
        sums.append(running)
    running = jnp.concatenate(sums, axis=1)
    got = lax.ppermute(running[half:], "ex", swap)
    moe_out = jnp.where(
        core == 0,
        jnp.concatenate([running[:half], got], axis=0),
        jnp.concatenate([got, running[:half]], axis=0),
    )
    return (resid + moe_out.astype(jnp.float32)).astype(jnp.bfloat16)[None]


def solution(mesh):
    return jax.shard_map(
        on_device,
        mesh=mesh,
        in_specs=(
            P("ex", None, None),
            P(),
            P(None, None, "kv"),
            P("kv", None),
            P("ex", None, None, "kv"),
            P("ex"),
            P(),
            P(None, None, "ex", "kv"),
            P("ex", "kv", None),
            P("ex", "kv", None),
        ),
        out_specs=P("ex", "kv", None),
        check_vma=False,
    )
```

```python
import functools
import math

import jax
import jax.numpy as jnp
from jax import lax
from jax.experimental import pallas as pl
from jax.experimental.pallas import tpu as pltpu
from jax.sharding import PartitionSpec as P

HD = 128
TOPK = 8
PLEN = 512
REQ_DEV = 2
QB = 32
CMAX = 512


def rms_scale(rows, gain):
    values = rows.astype(jnp.float32)
    scale = lax.rsqrt(jnp.mean(values * values, axis=-1, keepdims=True) + 1e-06)
    return values * scale * gain


def attention_kernel(scale, len_ref, x_ref, gain_ref, w_ref, cache_ref, w_out_ref, out_ref, normed):
    @pl.when(pl.program_id(0) == 0)
    def _():
        normed[...] = rms_scale(x_ref[...], gain_ref[...]).astype(jnp.bfloat16)
        out_ref[...] = jnp.zeros_like(out_ref)

    rows = normed[...]
    query, keys, values = (
        jnp.dot(rows, w_ref[j], preferred_element_type=jnp.float32).astype(jnp.bfloat16)
        for j in range(3)
    )

    def scores_of(q, k):
        return scale * lax.dot_general(
            q, k, (((1,), (1,)), ((), ())), preferred_element_type=jnp.float32
        )

    def mix(weights, v):
        return jnp.dot(weights.astype(jnp.bfloat16), v, preferred_element_type=jnp.float32)

    heads = []
    for head in range(query.shape[1] // HD):
        cut = slice(head * HD, (head + 1) * HD)
        q, k, v = query[:, cut], keys[:, cut], values[:, cut]
        scores = scores_of(q[:PLEN], k[:PLEN])
        weights = jnp.exp(scores - jnp.max(scores, axis=-1, keepdims=True))
        total = jnp.sum(weights, axis=-1, keepdims=True)
        outs = [(mix(weights, v[:PLEN]) / total).astype(jnp.bfloat16)]
        for request in range(REQ_DEV):
            own = slice(PLEN + request * QB, PLEN + (request + 1) * QB)
            fresh = scores_of(q[own], k[own])
            stored = scores_of(q[own], cache_ref[request, 0, :, cut])
            slots = lax.broadcasted_iota(jnp.int32, stored.shape, 1)
            stored = jnp.where(slots < len_ref[request], stored, -1e30)
            top = jnp.maximum(
                jnp.max(fresh, axis=-1, keepdims=True), jnp.max(stored, axis=-1, keepdims=True)
            )
            fresh, stored = jnp.exp(fresh - top), jnp.exp(stored - top)
            total = jnp.sum(fresh, axis=-1, keepdims=True) + jnp.sum(stored, axis=-1, keepdims=True)
            mixed = mix(fresh, v[own]) + mix(stored, cache_ref[request, 1, :, cut])
            outs.append((mixed / total).astype(jnp.bfloat16))
        heads.append(jnp.concatenate(outs, axis=0))
    out_ref[...] += jnp.dot(
        jnp.concatenate(heads, axis=1), w_out_ref[...], preferred_element_type=jnp.float32
    )


def attention(rows, gain, w_qkv, cache, cache_len, w_out):
    count, width = rows.shape
    units = w_qkv.shape[2]
    block = min(2 * HD, units)
    return pl.pallas_call(
        functools.partial(attention_kernel, 1.0 / math.sqrt(HD)),
        grid=(units // block,),
        in_specs=[
            pl.BlockSpec(memory_space=pltpu.SMEM),
            pl.BlockSpec((count, width), lambda i: (0, 0)),
            pl.BlockSpec((1, width), lambda i: (0, 0)),
            pl.BlockSpec((3, width, block), lambda i: (0, 0, i)),
            pl.BlockSpec((REQ_DEV, 2, CMAX, block), lambda i: (0, 0, 0, i)),
            pl.BlockSpec((block, width), lambda i: (i, 0)),
        ],
        out_specs=pl.BlockSpec((count, width), lambda i: (0, 0)),
        out_shape=jax.ShapeDtypeStruct((count, width), jnp.float32),
        scratch_shapes=[pltpu.VMEM((count, width), jnp.bfloat16)],
        compiler_params=pltpu.CompilerParams(vmem_limit_bytes=38 * 1024 * 1024),
        cost_estimate=pl.CostEstimate(
            flops=8 * count * width * units + 4 * PLEN * PLEN * units,
            bytes_accessed=8 * width * units + 6 * count * width,
            transcendentals=PLEN * PLEN * units // HD,
        ),
        name="attention",
    )(cache_len, rows, gain[None], jnp.transpose(w_qkv, (1, 0, 2)), cache, w_out)


def share_columns(share):
    high = share.astype(jnp.bfloat16)
    low = (share - high.astype(jnp.float32)).astype(jnp.bfloat16)
    spare = -2 * share.shape[1] % 128
    return jnp.concatenate([high, low, jnp.zeros((share.shape[0], spare), jnp.bfloat16)], axis=1)


def hidden_kernel(experts, width, me_ref, *refs):
    x_refs, weight_refs, out_refs = refs[:2], refs[2:-2], refs[-2:]
    units = weight_refs[0].shape[2]
    me = me_ref[0]
    for x_ref, out_ref in zip(x_refs, out_refs):
        extra = x_ref[:, width:].astype(jnp.float32)
        lanes = lax.broadcasted_iota(jnp.int32, extra.shape, 1)
        mine = (lanes == me) | (lanes == me + experts)
        share = jnp.sum(jnp.where(mine, extra, 0.0), axis=-1, keepdims=True)
        for part in range(len(weight_refs) // 2):
            gate_w, up_w = (r[...].reshape(width, units) for r in weight_refs[2 * part : 2 * part + 2])
            x = x_ref[:, :width]
            gate = jnp.dot(x, gate_w, preferred_element_type=jnp.float32)
            up = jnp.dot(x, up_w, preferred_element_type=jnp.float32)
            gate = 0.5 * gate
            out_ref[:, part * units : (part + 1) * units] = (
                (gate + gate * jnp.tanh(gate)) * (up * share)
            ).astype(jnp.bfloat16)


def expert_hidden(experts, me, blocks, weights):
    count = blocks[0].shape[0]
    sources, slice_width, units = weights[0].shape
    width, hidden = sources * slice_width, units * len(weights) // 2
    vmem = pl.BlockSpec(memory_space=pltpu.VMEM)
    out = jax.ShapeDtypeStruct((count, hidden), jnp.bfloat16)
    return pl.pallas_call(
        functools.partial(hidden_kernel, experts, width),
        in_specs=[pl.BlockSpec(memory_space=pltpu.SMEM)] + [vmem] * (2 + len(weights)),
        out_specs=[vmem] * 2,
        out_shape=[out, out],
        compiler_params=pltpu.CompilerParams(vmem_limit_bytes=8 * 1024 * 1024),
        cost_estimate=pl.CostEstimate(
            flops=8 * count * width * hidden,
            bytes_accessed=4 * count * (width + hidden) + 4 * width * hidden,
            transcendentals=2 * count * hidden,
        ),
        name="expert_hidden",
    )(me, *blocks, *weights)


def down_kernel(*refs):
    hidden_refs, weight_refs, out_refs = refs[:2], refs[2:-2], refs[-2:]
    sources, slice_width, units = weight_refs[0].shape
    group = max(1, min(sources, 1024 // slice_width))
    for hidden_ref, out_ref in zip(hidden_refs, out_refs):
        for first in range(0, sources, group):
            total = None
            for part, weight_ref in enumerate(weight_refs):
                term = lax.dot_general(
                    hidden_ref[:, part * units : (part + 1) * units],
                    weight_ref[first : first + group].reshape(group * slice_width, units),
                    (((1,), (1,)), ((), ())),
                    preferred_element_type=jnp.float32,
                )
                total = term if total is None else total + term
            cut = slice(first * slice_width, (first + group) * slice_width)
            out_ref[:, cut] = total.astype(jnp.bfloat16)


def expert_down(hiddens, weights):
    count, hidden = hiddens[0].shape
    width = weights[0].shape[0] * weights[0].shape[1]
    vmem = pl.BlockSpec(memory_space=pltpu.VMEM)
    out = jax.ShapeDtypeStruct((count, width), jnp.bfloat16)
    return pl.pallas_call(
        down_kernel,
        in_specs=[vmem] * (2 + len(weights)),
        out_specs=[vmem] * 2,
        out_shape=[out, out],
        compiler_params=pltpu.CompilerParams(vmem_limit_bytes=8 * 1024 * 1024),
        cost_estimate=pl.CostEstimate(
            flops=4 * count * width * hidden,
            bytes_accessed=4 * count * (width + hidden) + 2 * width * hidden,
            transcendentals=0,
        ),
        name="expert_down",
    )(*hiddens, *weights)


def sum_kernel(cut, refs):
    total = refs[0][:, cut].astype(jnp.float32) + refs[1][:, cut].astype(jnp.float32)
    for ref in refs[2:-1]:
        total = total + ref[...].astype(jnp.float32)
    refs[-1][...] = total.astype(jnp.bfloat16)


def add_terms(cut, keep, got, running):
    terms = [keep, got] + ([] if running is None else [running])
    columns = cut.stop - cut.start
    vmem = pl.BlockSpec(memory_space=pltpu.VMEM)
    return pl.pallas_call(
        lambda *refs: sum_kernel(cut, refs),
        in_specs=[vmem] * len(terms),
        out_specs=vmem,
        out_shape=jax.ShapeDtypeStruct((keep.shape[0], columns), jnp.bfloat16),
        compiler_params=pltpu.CompilerParams(vmem_limit_bytes=8 * 1024 * 1024),
        cost_estimate=pl.CostEstimate(
            flops=2 * keep.shape[0] * columns,
            bytes_accessed=8 * keep.shape[0] * columns,
            transcendentals=0,
        ),
        name="add_terms",
    )(*terms)


def chip_ring(chips):
    rows = 4
    columns = chips // rows
    if chips % rows or columns < 2:
        return list(range(chips))
    order = [z * columns for z in range(rows)]
    for turn, z in enumerate(reversed(range(rows))):
        line = [z * columns + x for x in range(1, columns)]
        order += line if turn % 2 == 0 else line[::-1]
    return order


def on_device(
    x_tokens,
    attn_gain,
    w_qkv,
    w_out,
    cache,
    cache_len,
    moe_gain,
    w_trainer,
    expert_ids,
    route_probs,
):
    kv, ex = lax.axis_size("kv"), lax.axis_size("ex")
    me, me_kv = lax.axis_index("ex"), lax.axis_index("kv")
    experts = w_trainer.shape[0]

    def over_experts(part):
        return lax.all_to_all(part, "ex", split_axis=0, concat_axis=0, tiled=True)

    def over_kv(part):
        return [
            lax.ppermute(part, "kv", [(i, (i + turn) % kv) for i in range(kv)])
            for turn in range(1, kv)
        ]

    probs = route_probs[0]
    share = probs / jnp.sum(probs, axis=-1, keepdims=True)
    named = expert_ids[0][:, :, None] == jnp.arange(experts, dtype=jnp.int32)[None, None, :]
    factor = jnp.sum(jnp.where(named, share[:, :, None], 0.0), axis=1)
    factor = share_columns(factor)

    rows = x_tokens[0]
    row_count = rows.shape[0]
    rows_dev = row_count // kv
    gate = w_trainer[:, 0].astype(jnp.bfloat16)
    gate, rest = lax.optimization_barrier((gate, w_trainer))
    up, down = (rest[:, kind].astype(jnp.bfloat16) for kind in (1, 2))
    gate = over_experts(gate)
    mixed = attention(rows, attn_gain, w_qkv, cache, cache_len, w_out)
    mixed, gate, up, down = lax.optimization_barrier((mixed, gate, up, down))
    gates = over_kv(gate)
    up = over_experts(up)
    mixed = mixed.reshape(kv, rows_dev, mixed.shape[1])

    def rows_of(part):
        return lax.dynamic_index_in_dim(mixed, part, 0, keepdims=False)

    own_rows = lax.dynamic_slice_in_dim(rows, me_kv * rows_dev, rows_dev, 0)
    resid = own_rows.astype(jnp.float32) + rows_of(me_kv)
    for turn in range(1, kv):
        sent = rows_of(lax.rem(me_kv + turn, kv)).astype(jnp.bfloat16)
        sent = lax.ppermute(sent, "kv", [(i, (i + turn) % kv) for i in range(kv)])
        resid = resid + sent.astype(jnp.float32)
    resid, up, down = lax.optimization_barrier((resid, up, down))
    ups = over_kv(up)
    down = over_experts(down)
    moe_in = rms_scale(resid, moe_gain).astype(jnp.bfloat16)
    moe_in = jnp.concatenate([moe_in, factor], axis=1)
    moe_in, gates = lax.optimization_barrier((moe_in, gates))

    cores = 2
    order = chip_ring(ex // cores)
    chips = len(order)
    half = rows_dev // 2
    core = lax.rem(me, cores)
    ring, swap = [], [(i, i ^ 1) for i in range(ex)]
    for spot, chip in enumerate(order):
        for c in range(cores):
            here = chip * cores + c
            ring.append((here, order[(spot + 1 - 2 * c) % chips] * cores + c))

    def half_of(array, which):
        return lax.dynamic_slice_in_dim(array, which * half, half, 0)

    got = lax.ppermute(half_of(moe_in, 1 - core), "ex", swap)
    held = jnp.concatenate([half_of(moe_in, core), got], axis=0)
    first_weights = [gate, up]
    due = {3: [0, 1], 4: [2, 3], 5: [4], 6: [5], 7: [6]}
    blocks, hiddens = [held], {}

    def hidden_of(step):
        other = lax.ppermute(blocks[step], "ex", swap)
        return expert_hidden(experts, me[None], [blocks[step], other], first_weights)

    for step in range(1, chips):
        held = lax.ppermute(held, "ex", ring)
        if step == 1:
            held, down = lax.optimization_barrier((held, down))
            downs = over_kv(down)
        if step == 2:
            held, ups = lax.optimization_barrier((held, ups))
            for pair in zip(gates, ups):
                first_weights += pair
        blocks.append(held)
        for early in due.get(step, []):
            hiddens[early] = hidden_of(early)
            held, hiddens[early] = lax.optimization_barrier((held, hiddens[early]))
        if step == min(4, chips - 1):
            held, downs = lax.optimization_barrier((held, downs))
        blocks[step] = held
    for step in range(chips):
        if step not in hiddens:
            hiddens[step] = hidden_of(step)
    hiddens = [hiddens[step] for step in range(chips)]
    keeps, gots = [], []
    for pair in hiddens:
        keep, give = expert_down(pair, [down] + downs)
        keeps.append(keep)
        gots.append(lax.ppermute(give, "ex", swap))

    width = w_out.shape[1]
    sums = []
    for cut in (slice(0, width // 2), slice(width // 2, width)):
        running = None
        for step in list(range(1, chips)) + [0]:
            running = add_terms(cut, keeps[step], gots[step], running)
            if step:
                running = lax.ppermute(running, "ex", ring)
        sums.append(running)
    running = jnp.concatenate(sums, axis=1)
    got = lax.ppermute(running[half:], "ex", swap)
    moe_out = jnp.where(
        core == 0,
        jnp.concatenate([running[:half], got], axis=0),
        jnp.concatenate([got, running[:half]], axis=0),
    )
    return (resid + moe_out.astype(jnp.float32)).astype(jnp.bfloat16)[None]


def solution(mesh):
    return jax.shard_map(
        on_device,
        mesh=mesh,
        in_specs=(
            P("ex", None, None),
            P(),
            P(None, None, "kv"),
            P("kv", None),
            P("ex", None, None, "kv"),
            P("ex"),
            P(),
            P(None, None, "ex", "kv"),
            P("ex", "kv", None),
            P("ex", "kv", None),
        ),
        out_specs=P("ex", "kv", None),
        check_vma=False,
    )
```
